128 devices in a mesh: lon: 8 (over x, core), lat: 16 (over z, y).
Axes of the slice: x: 4, y: 4, z: 4, core: 2. Of those that a mesh axis runs over, the one named last changes fastest.
Arguments:
- tokens: bfloat16 [4, 64, 128, 1024], P(None, 'lon', 'lat'), may hold values from -6 to 6
- cotangent: bfloat16 [4, 64, 128, 1024], P(None, 'lon', 'lat'), may hold values from -6 to 6
- attention_in: bfloat16 [1024, 3072], replicated
- attention_out: bfloat16 [1024, 1024], replicated, may hold values from -0.1875 to 0.1875
- norm_attention: float32 [1024], replicated, may hold values from 0.25 to 1.75
- norm_expert: float32 [1024], replicated, may hold values from 0.25 to 1.75
- expert_up: bfloat16 [32, 1024, 4096], P('lon', None, 'lat'), may hold values from -0.1875 to 0.1875
- expert_down: bfloat16 [32, 4096, 1024], P('lon', 'lat'), may hold values from -0.09375 to 0.09375
- route_gain: float32 [4, 64, 128], P(None, 'lon', 'lat'), may hold values from 0.5 to 2
- assignment: int32 [4, 64, 128], P(None, 'lon', 'lat'), may hold values from 0 to 7, as said below
- slot_index: int32 [4, 64, 128], P(None, 'lon', 'lat'), may hold values from 0 to 15, as said below
Outputs:
- grad_tokens: bfloat16 [4, 64, 128, 1024], P(None, 'lon', 'lat')
- grad_up: float32 [32, 1024, 4096], P('lon', None, 'lat')
- grad_down: float32 [32, 4096, 1024], P('lon', 'lat')
The draws below stay inside these ranges and needn't reach their ends.
Inputs may be any that keep to these rules, and one draw needn't show every extreme that they name: `assignment`: among the rows of one device and one variable group (8 x 8 cells, aligned blocks), no expert is named more than 16 times, and one is named exactly 16 times. `slot_index`: rows of one device and one variable group that name the same expert have distinct slots.
All inputs are finite; a program needn't handle non-finite values.
Results may differ from the reference program's by a relative error of at most 0.02.
Values may be sent and summed in bfloat16 or wider, within the bound.
No kernel may reach another device: no remote copies, remote signals or barrier semaphores. Data moves between devices by JAX's collectives and lax.ppermute only.
A program may use at most 320 MiB of HBM per device.

```python
import math
import jax
import jax.numpy as jnp
from jax import lax

D = 1024
HS = 64
FF = 4096
EPG = 8
GROUPS = 4
WIN = 8
LONB = 8
LATB = 8
CAP = 16
EXPERTS = 32
NLON = 64
NLAT = 128
N_LON = 8
N_LAT = 16


def routing_tables(key):
    key_hot, key_rows = jax.random.split(key, 2)
    blocks_lon = NLON // LONB
    blocks_lat = NLAT // LATB
    block_count = GROUPS * blocks_lon * blocks_lat
    block_rows = LONB * LATB
    hot_group = jax.random.randint(key_hot, (GROUPS,), 0, EPG)
    hot_block = jnp.repeat(hot_group, blocks_lon * blocks_lat)
    candidates = jnp.repeat(jnp.arange(EPG - 1, dtype=jnp.int32), CAP)

    def slot_perm(sub_key):
        return jax.random.permutation(sub_key, CAP)

    def one_block(block_key, hot_expert):
        key_pick, key_order, key_slot = jax.random.split(block_key, 3)
        picks = jax.random.permutation(key_pick, candidates)[:block_rows - CAP]
        others = picks + (picks >= hot_expert).astype(jnp.int32)
        experts = jnp.concatenate([jnp.full((CAP,), hot_expert, jnp.int32), others])
        experts = jax.random.permutation(key_order, experts)
        onehot = (experts[:, None] == jnp.arange(EPG, dtype=jnp.int32)[None, :]).astype(jnp.int32)
        rank = jnp.sum((jnp.cumsum(onehot, 0) - onehot) * onehot, 1)
        perms = jax.vmap(slot_perm)(jax.random.split(key_slot, EPG))
        slots = perms[experts, rank].astype(jnp.int32)
        return (experts, slots)
    experts, slots = jax.vmap(one_block)(jax.random.split(key_rows, block_count), hot_block)

    def to_grid(table):
        table = table.reshape(GROUPS, blocks_lon, blocks_lat, LONB, LATB)
        return table.transpose(0, 1, 3, 2, 4).reshape(GROUPS, NLON, NLAT)
    return (to_grid(experts), to_grid(slots))


def draw_assignment(key, part):
    return routing_tables(key)[0]


def draw_slot_index(key, part):
    return routing_tables(key)[1]


def draw_attention_in(key, part):
    key = jax.random.fold_in(key, 17)
    key_base = jax.random.fold_in(key, 0)
    base = jax.random.normal(key_base, (D, 3 * D), jnp.float32) * D ** (-0.5)
    return base.astype(jnp.bfloat16)


def level_of(own_key, extent, shards, low, largest):
    factor_of = 1.0
    for dim, shards_of in shards:
        steps = jax.random.uniform(jax.random.fold_in(jax.random.fold_in(own_key, 6), dim), (shards_of,), jnp.float32, low / len(shards), largest / len(shards))
        factor_of = factor_of * jnp.repeat(jnp.exp(steps), extent[dim] // shards_of).reshape((-1,) + (1,) * (len(extent) - 1 - dim))
    return factor_of


def normal_values(stream_key, extent, width, limit, cuts=(), kind=jnp.bfloat16):
    drawn = width * jax.random.normal(stream_key, extent, jnp.float32)
    if cuts:
        drawn = drawn * level_of(stream_key, extent, cuts, -0.22, 0.18)
    return jnp.clip(drawn, -limit, limit).astype(kind)


def setup_inputs(seed: int = 0) -> dict:
    seeds = jax.random.split(jax.random.key(seed), 12)
    tokens = normal_values(seeds[0], (GROUPS, NLON, NLAT, D), 1.0, 6.0, ((1, 8), (2, 16)))
    cotangent = normal_values(seeds[1], (GROUPS, NLON, NLAT, D), 1.0, 6.0, ((1, 8), (2, 16)))
    attention_in = draw_attention_in(jax.random.fold_in(seeds[11], 71), 0)
    attention_out = normal_values(seeds[3], (D, D), D ** -0.5, 0.1875)
    norm_attention = jnp.clip(1.0 + 0.15 * jax.random.normal(seeds[4], (D,), jnp.float32), 0.25, 1.75)
    norm_expert = jnp.clip(1.0 + 0.15 * jax.random.normal(seeds[5], (D,), jnp.float32), 0.25, 1.75)
    expert_up = normal_values(seeds[6], (EXPERTS, D, FF), D ** -0.5, 0.1875, ((0, 8), (2, 16)))
    expert_down = normal_values(seeds[7], (EXPERTS, FF, D), FF ** -0.5, 0.09375, ((0, 8), (1, 16)))
    route_gain = jnp.clip(jnp.exp(math.log(2.0) - 1.3862944 * jax.random.uniform(seeds[8], (GROUPS, NLON, NLAT), jnp.float32) ** level_of(seeds[8], (GROUPS, NLON, NLAT), ((1, 8), (2, 16)), -0.2, 0.2)), 0.5, 2.0)
    assignment = draw_assignment(jax.random.fold_in(seeds[11], 71), 0)
    slot_index = draw_slot_index(jax.random.fold_in(seeds[11], 71), 0)
    return dict(tokens=tokens, cotangent=cotangent, attention_in=attention_in, attention_out=attention_out, norm_attention=norm_attention, norm_expert=norm_expert, expert_up=expert_up, expert_down=expert_down, route_gain=route_gain, assignment=assignment, slot_index=slot_index)


EPSILON = 1e-06
TANH_SCALE = math.sqrt(2.0 / math.pi)
CUBIC_COEF = 0.044715
MASKED = -1000000000.0

def gelu_parts(preact):
    argument = TANH_SCALE * (preact + CUBIC_COEF * preact * preact * preact)
    tangent = jnp.tanh(argument)
    activated = 0.5 * preact * (1.0 + tangent)
    derivative = 0.5 * (1.0 + tangent) + 0.5 * preact * (1.0 - tangent * tangent) * TANH_SCALE * (1.0 + 3.0 * CUBIC_COEF * preact * preact)
    return (activated, derivative)

def norm_rows(grid_field, gain_vec):
    values_f = grid_field.astype(jnp.float32)
    factor = lax.rsqrt(lax.optimization_barrier(jnp.mean(values_f * values_f, -1, keepdims=True)) + EPSILON)
    return values_f * factor * gain_vec

def norm_back(grid_field, gain_vec, grad_in):
    values_f = grid_field.astype(jnp.float32)
    factor = lax.rsqrt(lax.optimization_barrier(jnp.mean(values_f * values_f, -1, keepdims=True)) + EPSILON)
    scaled_grad = grad_in * gain_vec
    inner_mean = lax.optimization_barrier(jnp.mean(values_f * scaled_grad, -1, keepdims=True))
    return factor * scaled_grad - values_f * factor * factor * factor * inner_mean

def to_windows(grid_field, side):
    groups_n, rows_a, rows_b, features = grid_field.shape
    blocked = grid_field.reshape(groups_n, rows_a // side, side, rows_b // side, side, features)
    return blocked.transpose(0, 1, 3, 2, 4, 5).reshape(-1, side * side, features)

def from_windows(blocks, shape, side):
    groups_n, rows_a, rows_b, features = shape
    blocked = blocks.reshape(groups_n, rows_a // side, rows_b // side, side, side, features)
    return blocked.transpose(0, 1, 3, 2, 4, 5).reshape(shape)

def attention_forward(rolled, region, weight_in, weight_out, gain_vec):
    normed = norm_rows(rolled, gain_vec).astype(jnp.bfloat16)
    blocks = to_windows(normed, WIN)
    windows_n, window_len, features = blocks.shape
    head_count = features // HS
    projected = jnp.dot(blocks.reshape(-1, features), weight_in, preferred_element_type=jnp.float32)
    projected = projected.astype(jnp.bfloat16).reshape(windows_n, window_len, 3, head_count, HS)
    queries = projected[:, :, 0].astype(jnp.float32)
    keyset = projected[:, :, 1].astype(jnp.float32)
    valueset = projected[:, :, 2].astype(jnp.float32)
    scores = jnp.einsum('wqhe,wkhe->whqk', queries, keyset) * HS ** (-0.5)
    zone_ids = to_windows(region[..., None], WIN)[..., 0]
    allowed = zone_ids[:, None, :, None] == zone_ids[:, None, None, :]
    scores = jnp.where(allowed, scores, MASKED)
    row_max = lax.optimization_barrier(jnp.max(scores, -1, keepdims=True))
    weights_exp = jnp.exp(scores - row_max)
    prob_full = weights_exp / lax.optimization_barrier(jnp.sum(weights_exp, -1, keepdims=True))
    prob_low = prob_full.astype(jnp.bfloat16)
    attended = jnp.einsum('whqk,wkhe->wqhe', prob_low.astype(jnp.float32), valueset)
    attended = attended.astype(jnp.bfloat16).reshape(-1, features)
    output = jnp.dot(attended, weight_out, preferred_element_type=jnp.float32).astype(jnp.bfloat16)
    output = from_windows(output.reshape(windows_n, window_len, features), rolled.shape, WIN)
    return (output, (queries, keyset, valueset, prob_full, prob_low))

def attention_backward(saved, grad_rolled, rolled, weight_in, weight_out, gain_vec):
    queries, keyset, valueset, prob_full, prob_low = saved
    windows_n = prob_full.shape[0]
    window_len = prob_full.shape[2]
    features = weight_out.shape[0]
    grad_rows = to_windows(grad_rolled, WIN).reshape(-1, features)
    grad_att = jnp.dot(grad_rows, weight_out.T, preferred_element_type=jnp.float32).astype(jnp.bfloat16)
    grad_att = grad_att.reshape(windows_n, window_len, -1, HS).astype(jnp.float32)
    grad_probs = jnp.einsum('wqhe,wkhe->whqk', grad_att, valueset)
    grad_values = jnp.einsum('whqk,wqhe->wkhe', prob_low.astype(jnp.float32), grad_att)
    grad_scores = prob_full * (grad_probs - lax.optimization_barrier(jnp.sum(prob_full * grad_probs, -1, keepdims=True)))
    scaled = (grad_scores * HS ** (-0.5)).astype(jnp.bfloat16).astype(jnp.float32)
    grad_queries = jnp.einsum('whqk,wkhe->wqhe', scaled, keyset)
    grad_keys = jnp.einsum('whqk,wqhe->wkhe', scaled, queries)
    stacked = jnp.stack([grad_queries, grad_keys, grad_values], 2).astype(jnp.bfloat16).reshape(-1, 3 * features)
    grad_norm = jnp.dot(stacked, weight_in.T, preferred_element_type=jnp.float32)
    grad_norm = from_windows(grad_norm.reshape(windows_n, window_len, features), rolled.shape, WIN)
    return norm_back(rolled, gain_vec, grad_norm).astype(jnp.bfloat16)

def expert_terms(packed):
    rows_in, rows_grad, weight_up, weight_down = packed
    preact = jnp.dot(rows_in, weight_up, preferred_element_type=jnp.float32)
    activated, derivative = gelu_parts(preact)
    hidden = activated.astype(jnp.bfloat16)
    grad_hidden = jnp.dot(rows_grad, weight_down.T, preferred_element_type=jnp.float32)
    grad_pre = (grad_hidden * derivative).astype(jnp.bfloat16)
    part_down = jnp.dot(hidden.T, rows_grad, preferred_element_type=jnp.float32)
    part_up = jnp.dot(rows_in.T, grad_pre, preferred_element_type=jnp.float32)
    returned_part = jnp.dot(grad_pre, weight_up.T, preferred_element_type=jnp.float32).astype(jnp.bfloat16)
    return (part_up, part_down, returned_part)

def reference(tokens, cotangent, attention_in, attention_out, norm_attention, norm_expert, expert_up, expert_down, route_gain, assignment, slot_index):
    shift_rows = WIN // 2
    rolled = jnp.roll(tokens, (-shift_rows, -shift_rows), axis=(1, 2))
    lat_rolled = jnp.arange(NLAT, dtype=jnp.int32)
    region = jnp.broadcast_to((lat_rolled >= NLAT - shift_rows).astype(jnp.int32)[None, None, :], (GROUPS, NLON, NLAT))
    produced, saved = attention_forward(rolled, region, attention_in, attention_out, norm_attention)
    attended = jnp.roll(produced, (shift_rows, shift_rows), axis=(1, 2))
    middle = (tokens.astype(jnp.float32) + attended.astype(jnp.float32)).astype(jnp.bfloat16)
    normed = norm_rows(middle, norm_expert).astype(jnp.bfloat16)
    grad_out = (route_gain[..., None] * cotangent.astype(jnp.float32)).astype(jnp.bfloat16)
    lon_pos = jnp.arange(NLON, dtype=jnp.int32)[None, :, None]
    lat_pos = jnp.arange(NLAT, dtype=jnp.int32)[None, None, :]
    device_ids = lon_pos // LONB * N_LAT + lat_pos // LATB
    group_ids = jnp.arange(GROUPS, dtype=jnp.int32)[:, None, None]
    expert_id = (group_ids * EPG + assignment).reshape(-1)
    position = (device_ids * CAP + slot_index).reshape(-1)
    buffer_len = N_LON * N_LAT * CAP
    buf_in = jnp.zeros((EXPERTS, buffer_len, D), jnp.bfloat16).at[expert_id, position].set(normed.reshape(-1, D))
    buf_grad = jnp.zeros((EXPERTS, buffer_len, D), jnp.bfloat16).at[expert_id, position].set(grad_out.reshape(-1, D))
    grad_up, grad_down, returned_all = lax.map(expert_terms, (buf_in, buf_grad, expert_up, expert_down))
    grad_normed = returned_all[expert_id, position].reshape(GROUPS, NLON, NLAT, D)
    grad_middle = cotangent.astype(jnp.float32) + norm_back(middle, norm_expert, grad_normed.astype(jnp.float32))
    grad_middle = grad_middle.astype(jnp.bfloat16)
    grad_rolled = jnp.roll(grad_middle, (-shift_rows, -shift_rows), axis=(1, 2))
    branch = attention_backward(saved, grad_rolled, rolled, attention_in, attention_out, norm_attention)
    branch = jnp.roll(branch, (shift_rows, shift_rows), axis=(1, 2))
    grad_tokens = (grad_middle.astype(jnp.float32) + branch.astype(jnp.float32)).astype(jnp.bfloat16)
    return (grad_tokens, grad_up, grad_down)
```

```python
import functools
import math

import jax
import jax.numpy as jnp
from jax import lax
from jax.experimental import pallas as pl
from jax.experimental.pallas import tpu as pltpu
from jax.sharding import PartitionSpec as P

HS = 64
EPG = 8
WIN = 8
EPSILON = 1e-06
TANH_SCALE = math.sqrt(2.0 / math.pi)
CUBIC_COEF = 0.044715
MASKED = -1000000000.0

DIRECTIONS = (1, 4, 3, 12)
PARTS = 4
ROWS = 64
SHARD = 272
TILE = 256
CHUNK = 16
TILE_CHUNKS = 24
TILES = 8
BLOCK = 256
BLOCKS = 20
SPARE = 19 * (BLOCK // CHUNK)
BUFFER = BLOCKS * BLOCK


def cube_masks(part):
    masks = [0]
    for step in range(4):
        direction = DIRECTIONS[(part + step) % 4]
        masks += [m ^ direction for m in masks]
    return masks


def swapped(block, axis, direction):
    return lax.ppermute(block, axis, [(i, i ^ direction) for i in range(lax.axis_size(axis))])


def turned(block, distance):
    devices = lax.axis_size("lon")
    return lax.ppermute(block, "lon", [(i, (i + distance) % devices) for i in range(devices)])


def moved(block, lon_step, lat_step):
    lons, lats = lax.axis_size("lon"), lax.axis_size("lat")
    route = [
        (i * lats + j, (i + lon_step) % lons * lats + (j + lat_step) % lats)
        for i in range(lons)
        for j in range(lats)
    ]
    return lax.ppermute(block, ("lon", "lat"), route)


def gelu_parts(preact):
    argument = TANH_SCALE * (preact + CUBIC_COEF * preact * preact * preact)
    tangent = jnp.tanh(argument)
    activated = 0.5 * preact * (1.0 + tangent)
    derivative = 0.5 * (1.0 + tangent) + 0.5 * preact * (1.0 - tangent * tangent) * TANH_SCALE * (
        1.0 + 3.0 * CUBIC_COEF * preact * preact
    )
    return (activated, derivative)


def norm_rows(field, gain_vec):
    values_f = field.astype(jnp.float32)
    factor = lax.rsqrt(jnp.mean(values_f * values_f, -1, keepdims=True) + EPSILON)
    return values_f * factor * gain_vec


def norm_back(field, gain_vec, grad_in):
    values_f = field.astype(jnp.float32)
    factor = lax.rsqrt(jnp.mean(values_f * values_f, -1, keepdims=True) + EPSILON)
    scaled_grad = grad_in * gain_vec
    inner_mean = jnp.mean(values_f * scaled_grad, -1, keepdims=True)
    return factor * scaled_grad - values_f * factor * factor * factor * inner_mean


def dot_f32(a, b, contract=((1,), (0,))):
    return lax.dot_general(a, b, (contract, ((), ())), preferred_element_type=jnp.float32)


def block_rows(index):
    return pl.ds(pl.multiple_of(index * BLOCK, BLOCK), BLOCK)


def chunk_rows(index):
    return pl.ds(pl.multiple_of(index * CHUNK, CHUNK), CHUNK)


def clear_blocks(buffer, count):
    def clear(b, carry):
        buffer[block_rows(b), :] = jnp.zeros((BLOCK, buffer.shape[1]), buffer.dtype)
        return carry

    lax.fori_loop(0, count, clear, 0)


def compact_tile(t, tile, place_ref, slots_row_ref, buffer):
    spots = lax.broadcasted_iota(jnp.int32, (TILE_CHUNKS * CHUNK, TILE), 0)
    pick = (spots == slots_row_ref[t : t + 1, :]).astype(jnp.bfloat16)
    packed = dot_f32(pick, tile).astype(jnp.bfloat16)
    for q in range(TILE_CHUNKS):
        buffer[chunk_rows(place_ref[t, q]), :] = packed[q * CHUNK : (q + 1) * CHUNK]


def grad_kernel(place_ref, plan_ref, offset_ref, rows_ref, own_ref, other_ref, slots_row_ref,
                packed_ref, hidden_ref, raw, weights, packed, hidden, raw_sem, weight_sem, packed_sem, hidden_sem):
    count = plan_ref[BLOCKS]
    loads = []
    for i in range(4 * TILES):
        start = pl.multiple_of(offset_ref[i], CHUNK)
        loads.append(pltpu.make_async_copy(rows_ref.at[pl.ds(start, ROWS)], raw.at[pl.ds(i * ROWS, ROWS)], raw_sem.at[i]))
    for load in loads:
        load.start()
    weight_loads = [
        pltpu.make_async_copy(own_ref, weights.at[pl.ds(0, 4)], weight_sem.at[0]),
        pltpu.make_async_copy(other_ref, weights.at[pl.ds(4, 4)], weight_sem.at[1]),
    ]
    for load in weight_loads:
        load.start()
    clear_blocks(packed, count)
    for t in range(TILES):
        for load in loads[4 * t : 4 * t + 4]:
            load.wait()
        compact_tile(t, raw[t * TILE : (t + 1) * TILE, :], place_ref, slots_row_ref, packed)
    for load in weight_loads:
        load.wait()

    def stores(b):
        return (
            pltpu.make_async_copy(packed.at[block_rows(b)], packed_ref.at[block_rows(b)], packed_sem.at[b]),
            pltpu.make_async_copy(hidden.at[block_rows(b)], hidden_ref.at[block_rows(b)], hidden_sem.at[b]),
        )

    def step(b, carry):
        weight = weights[plan_ref[b]]
        hidden[block_rows(b), :] = dot_f32(packed[block_rows(b), :], weight, ((1,), (1,)))
        for store in stores(b):
            store.start()
        return carry

    lax.fori_loop(0, count, step, 0)

    def finish(b, carry):
        for store in stores(b):
            store.wait()
        return carry

    lax.fori_loop(0, count, finish, 0)


def grad_side(place, plan, offsets, rows, own, other, slots_row):
    hidden_units = own.shape[1]
    features = own.shape[2]
    any_spec = pl.BlockSpec(memory_space=pl.ANY)
    smem = pl.BlockSpec(memory_space=pltpu.SMEM)
    return pl.pallas_call(
        grad_kernel,
        out_shape=(
            jax.ShapeDtypeStruct((BUFFER, features), jnp.bfloat16),
            jax.ShapeDtypeStruct((BUFFER, hidden_units), jnp.float32),
        ),
        in_specs=[smem, smem, smem, any_spec, any_spec, any_spec, pl.BlockSpec(memory_space=pltpu.VMEM)],
        out_specs=(any_spec, any_spec),
        scratch_shapes=[
            pltpu.VMEM((TILES * TILE, features), jnp.bfloat16),
            pltpu.VMEM((EPG, hidden_units, features), jnp.bfloat16),
            pltpu.VMEM((BUFFER, features), jnp.bfloat16),
            pltpu.VMEM((BUFFER, hidden_units), jnp.float32),
            pltpu.SemaphoreType.DMA((4 * TILES,)),
            pltpu.SemaphoreType.DMA((2,)),
            pltpu.SemaphoreType.DMA((BLOCKS,)),
            pltpu.SemaphoreType.DMA((BLOCKS,)),
        ],
        compiler_params=pltpu.CompilerParams(vmem_limit_bytes=40 * 2**20),
        cost_estimate=pl.CostEstimate(flops=6 * 10**9, bytes_accessed=24 * 2**20, transcendentals=0),
    )(place, plan, offsets, rows, own, other, slots_row)


def expert_kernel(place_ref, plan_ref, rows0_ref, rows1_ref, rows2_ref, rows3_ref, own_ref, other_ref, ghid_ref,
                  slots_row_ref, slots_col_ref,
                  back0_ref, back1_ref, back2_ref, back3_ref, packed_ref, hidden_ref, gpre_ref,
                  raw, weights, ghid, packed, result, hidden, gpre, back, stage,
                  raw_sem, weight_sem, ghid_sem, packed_sem, hidden_sem, gpre_sem, back_sem):
    count = plan_ref[BLOCKS]
    row_refs = (rows0_ref, rows1_ref, rows2_ref, rows3_ref)
    back_refs = (back0_ref, back1_ref, back2_ref, back3_ref)

    def half(t):
        return pl.ds(t % 2 * TILE, TILE)

    loads = [
        pltpu.make_async_copy(row_refs[t // 2].at[half(t)], raw.at[pl.ds(t * TILE, TILE)], raw_sem.at[t])
        for t in range(TILES)
    ]
    for load in loads:
        load.start()
    weight_loads = [
        pltpu.make_async_copy(own_ref, weights.at[pl.ds(0, 4)], weight_sem.at[0]),
        pltpu.make_async_copy(other_ref, weights.at[pl.ds(4, 4)], weight_sem.at[1]),
    ]
    for load in weight_loads:
        load.start()

    def ghid_load(b):
        return pltpu.make_async_copy(ghid_ref.at[block_rows(b)], ghid.at[block_rows(b)], ghid_sem.at[b])

    def begin(b, carry):
        ghid_load(b).start()
        return carry

    lax.fori_loop(0, count, begin, 0)
    clear_blocks(packed, count)
    result[SPARE * CHUNK : (SPARE + 1) * CHUNK, :] = jnp.zeros((CHUNK, result.shape[1]), result.dtype)
    for t in range(TILES):
        loads[t].wait()
        compact_tile(t, raw[t * TILE : (t + 1) * TILE, :], place_ref, slots_row_ref, packed)
    for load in weight_loads:
        load.wait()

    def stores(b):
        return (
            pltpu.make_async_copy(packed.at[block_rows(b)], packed_ref.at[block_rows(b)], packed_sem.at[b]),
            pltpu.make_async_copy(hidden.at[block_rows(b)], hidden_ref.at[block_rows(b)], hidden_sem.at[b]),
            pltpu.make_async_copy(gpre.at[block_rows(b)], gpre_ref.at[block_rows(b)], gpre_sem.at[b]),
        )

    def step(b, carry):
        weight = weights[plan_ref[b]]
        ghid_load(b).wait()
        preact = dot_f32(packed[block_rows(b), :], weight)
        activated, derivative = gelu_parts(preact)
        hidden[block_rows(b), :] = activated.astype(jnp.bfloat16)
        grad_pre = (ghid[block_rows(b), :] * derivative).astype(jnp.bfloat16)
        gpre[block_rows(b), :] = grad_pre
        result[block_rows(b), :] = dot_f32(grad_pre, weight, ((1,), (1,))).astype(jnp.bfloat16)
        for store in stores(b):
            store.start()
        return carry

    lax.fori_loop(0, count, step, 0)

    backs = [
        pltpu.make_async_copy(back.at[pl.ds(t * TILE, TILE)], back_refs[t // 2].at[half(t)], back_sem.at[t])
        for t in range(TILES)
    ]
    spots = lax.broadcasted_iota(jnp.int32, (TILE, TILE_CHUNKS * CHUNK), 1)
    for t in range(TILES):
        for q in range(TILE_CHUNKS):
            stage[q * CHUNK : (q + 1) * CHUNK, :] = result[chunk_rows(place_ref[t, q]), :]
        pick = (spots == slots_col_ref[:, t : t + 1]).astype(jnp.bfloat16)
        back[t * TILE : (t + 1) * TILE, :] = dot_f32(pick, stage[...]).astype(jnp.bfloat16)
        backs[t].start()

    def finish(b, carry):
        for store in stores(b):
            store.wait()
        return carry

    lax.fori_loop(0, count, finish, 0)
    for store in backs:
        store.wait()


def expert_side(place, plan, rows, own, other, ghid, slots_row, slots_col):
    features, hidden_units = own.shape[1:]
    any_spec = pl.BlockSpec(memory_space=pl.ANY)
    smem = pl.BlockSpec(memory_space=pltpu.SMEM)
    vmem = pl.BlockSpec(memory_space=pltpu.VMEM)
    part = jax.ShapeDtypeStruct((2 * TILE, features), jnp.bfloat16)
    small = jax.ShapeDtypeStruct((BUFFER, hidden_units), jnp.bfloat16)
    blocks_sem = pltpu.SemaphoreType.DMA((BLOCKS,))
    tiles_sem = pltpu.SemaphoreType.DMA((TILES,))
    outs = pl.pallas_call(
        expert_kernel,
        out_shape=(part,) * 4 + (jax.ShapeDtypeStruct((BUFFER, features), jnp.bfloat16), small, small),
        in_specs=[smem, smem] + [any_spec] * 7 + [vmem, vmem],
        out_specs=(any_spec,) * 7,
        scratch_shapes=[
            pltpu.VMEM((TILES * TILE, features), jnp.bfloat16),
            pltpu.VMEM((EPG, features, hidden_units), jnp.bfloat16),
            pltpu.VMEM((BUFFER, hidden_units), jnp.float32),
            pltpu.VMEM((BUFFER, features), jnp.bfloat16),
            pltpu.VMEM((BUFFER, features), jnp.bfloat16),
            pltpu.VMEM((BUFFER, hidden_units), jnp.bfloat16),
            pltpu.VMEM((BUFFER, hidden_units), jnp.bfloat16),
            pltpu.VMEM((TILES * TILE, features), jnp.bfloat16),
            pltpu.VMEM((TILE_CHUNKS * CHUNK, features), jnp.bfloat16),
            tiles_sem,
            pltpu.SemaphoreType.DMA((2,)),
            blocks_sem,
            blocks_sem,
            blocks_sem,
            blocks_sem,
            tiles_sem,
        ],
        compiler_params=pltpu.CompilerParams(vmem_limit_bytes=52 * 2**20),
        cost_estimate=pl.CostEstimate(flops=10 * 10**9, bytes_accessed=32 * 2**20, transcendentals=10**6),
    )(place, plan, *rows, own, other, ghid, slots_row, slots_col)
    return (outs[:4], outs[4], outs[5], outs[6])


def weight_kernel(plan_ref, rows_ref, gpre_ref, hidden_ref, grad_ref, *refs):
    before, (up_ref, down_ref) = refs[:-2], refs[-2:]
    b = pl.program_id(0)

    @pl.when(b < plan_ref[BLOCKS])
    def _():
        first = jnp.logical_or(b == 0, plan_ref[b] != plan_ref[jnp.maximum(b - 1, 0)])

        @pl.when(first)
        def _():
            if before:
                up_ref[...] = before[0][...]
                down_ref[...] = before[1][...]
            else:
                up_ref[...] = jnp.zeros_like(up_ref)
                down_ref[...] = jnp.zeros_like(down_ref)

        up_ref[0] += dot_f32(rows_ref[...], gpre_ref[...], ((0,), (0,)))
        down_ref[0] += dot_f32(hidden_ref[...], grad_ref[...], ((0,), (0,)))


def weight_side(plan, rows, gpre, hidden, grads, before):
    features, hidden_units = rows.shape[1], hidden.shape[1]

    def at_block(b, plan_ref):
        return (jnp.minimum(b, plan_ref[BLOCKS] - 1), 0)

    def at_expert(b, plan_ref):
        return (plan_ref[jnp.minimum(b, plan_ref[BLOCKS] - 1)], 0, 0)

    up_spec = pl.BlockSpec((1, features, hidden_units), at_expert)
    down_spec = pl.BlockSpec((1, hidden_units, features), at_expert)
    return pl.pallas_call(
        weight_kernel,
        out_shape=(
            jax.ShapeDtypeStruct((EPG, features, hidden_units), jnp.float32),
            jax.ShapeDtypeStruct((EPG, hidden_units, features), jnp.float32),
        ),
        grid_spec=pltpu.PrefetchScalarGridSpec(
            num_scalar_prefetch=1,
            grid=(BLOCKS,),
            in_specs=[
                pl.BlockSpec((BLOCK, features), at_block),
                pl.BlockSpec((BLOCK, hidden_units), at_block),
                pl.BlockSpec((BLOCK, hidden_units), at_block),
                pl.BlockSpec((BLOCK, features), at_block),
            ]
            + ([up_spec, down_spec] if before else []),
            out_specs=(up_spec, down_spec),
        ),
        compiler_params=pltpu.CompilerParams(vmem_limit_bytes=32 * 2**20),
        cost_estimate=pl.CostEstimate(flops=4 * 10**9, bytes_accessed=32 * 2**20, transcendentals=0),
    )(plan, rows, gpre, hidden, grads, *before)


def routes(named):
    onehot = (named[..., None] == jnp.arange(EPG)).astype(jnp.bfloat16)
    earlier = jnp.tril(jnp.ones((TILE, TILE), jnp.bfloat16), -1)
    ranks = jnp.einsum("rs,tse->tre", earlier, onehot, preferred_element_type=jnp.float32)
    onehot_f = onehot.astype(jnp.float32)
    rank = jnp.sum(ranks * onehot_f, -1).astype(jnp.int32)
    counts = jnp.sum(onehot_f, 1).astype(jnp.int32)
    chunks = (counts + CHUNK - 1) // CHUNK

    def before(values, axis):
        return jnp.cumsum(values, axis) - values

    starts = before(chunks, 1)
    slots = CHUNK * jnp.sum(onehot_f * starts[:, None, :].astype(jnp.float32), -1).astype(jnp.int32) + rank
    per_block = BLOCK // CHUNK
    blocks = jnp.maximum((jnp.sum(chunks, 0) + per_block - 1) // per_block, 1)
    first_block = before(blocks, 0)
    places = first_block[None, :] * per_block + before(chunks, 0)
    index = jnp.arange(TILE_CHUNKS)[None, :, None]
    inside = (index >= starts[:, None, :]) & (index < (starts + chunks)[:, None, :])
    place = jnp.sum(jnp.where(inside, places[:, None, :] + index - starts[:, None, :] - SPARE, 0), -1) + SPARE
    number = jnp.arange(BLOCKS)[:, None]
    plan = jnp.sum((number >= first_block[None, :]).astype(jnp.int32), -1) - 1
    plan = jnp.concatenate([plan, jnp.sum(blocks)[None]]).astype(jnp.int32)
    return (place.astype(jnp.int32), plan, slots, slots.T)


def attention_forward(rolled, zone_ids, weight_in, weight_out, gain_vec):
    normed = norm_rows(rolled, gain_vec).astype(jnp.bfloat16)
    windows_n, window_len, features = normed.shape
    head_count = features // HS
    projected = jnp.dot(normed.reshape(-1, features), weight_in, preferred_element_type=jnp.float32)
    projected = projected.astype(jnp.bfloat16).reshape(windows_n, window_len, 3, head_count, HS)
    queries = projected[:, :, 0]
    keyset = projected[:, :, 1]
    valueset = projected[:, :, 2]
    scores = jnp.einsum(
        "wqhe,wkhe->whqk", queries, keyset, preferred_element_type=jnp.float32
    ) * HS ** (-0.5)
    allowed = zone_ids[:, None] == zone_ids[None, :]
    scores = jnp.where(allowed, scores, MASKED)
    row_max = jnp.max(scores, -1, keepdims=True)
    weights_exp = jnp.exp(scores - row_max)
    prob_full = weights_exp / jnp.sum(weights_exp, -1, keepdims=True)
    prob_low = prob_full.astype(jnp.bfloat16)
    attended = jnp.einsum("whqk,wkhe->wqhe", prob_low, valueset, preferred_element_type=jnp.float32)
    attended = attended.astype(jnp.bfloat16).reshape(-1, features)
    output = jnp.dot(attended, weight_out, preferred_element_type=jnp.float32).astype(jnp.bfloat16)
    return (output.reshape(rolled.shape), (queries, keyset, valueset, prob_full, prob_low))


def attention_backward(saved, grad_rolled, rolled, weight_in, weight_out, gain_vec):
    queries, keyset, valueset, prob_full, prob_low = saved
    windows_n = prob_full.shape[0]
    window_len = prob_full.shape[2]
    features = weight_out.shape[0]
    grad_rows = grad_rolled.reshape(-1, features)
    grad_att = jnp.dot(grad_rows, weight_out.T, preferred_element_type=jnp.float32).astype(
        jnp.bfloat16
    )
    grad_att = grad_att.reshape(windows_n, window_len, -1, HS)
    grad_probs = jnp.einsum(
        "wqhe,wkhe->whqk", grad_att, valueset, preferred_element_type=jnp.float32
    )
    grad_values = jnp.einsum(
        "whqk,wqhe->wkhe", prob_low, grad_att, preferred_element_type=jnp.float32
    )
    grad_scores = prob_full * (grad_probs - jnp.sum(prob_full * grad_probs, -1, keepdims=True))
    scaled = (grad_scores * HS ** (-0.5)).astype(jnp.bfloat16)
    grad_queries = jnp.einsum("whqk,wkhe->wqhe", scaled, keyset, preferred_element_type=jnp.float32)
    grad_keys = jnp.einsum("whqk,wqhe->wkhe", scaled, queries, preferred_element_type=jnp.float32)
    stacked = (
        jnp.stack([grad_queries, grad_keys, grad_values], 2)
        .astype(jnp.bfloat16)
        .reshape(-1, 3 * features)
    )
    grad_norm = jnp.dot(stacked, weight_in.T, preferred_element_type=jnp.float32)
    return norm_back(rolled, gain_vec, grad_norm.reshape(rolled.shape)).astype(jnp.bfloat16)


def quadrants(field):
    half = WIN // 2
    cut = lambda a: a.reshape(a.shape[0], half * half, a.shape[-1])
    return (
        cut(field[:, half:, half:]),
        cut(field[:, half:, :half]),
        cut(field[:, :half, half:]),
        cut(field[:, :half, :half]),
    )


def roll_in(field):
    stays, lat_part, lon_part, both = quadrants(field)
    return jnp.concatenate(
        [stays, moved(lat_part, 0, -1), moved(lon_part, -1, 0), moved(both, -1, -1)], 1
    )


def roll_out(field):
    half = WIN // 2
    cells = half * half
    pieces = [field[:, i * cells : (i + 1) * cells] for i in range(4)]
    lat_part, lon_part, both = moved(pieces[1], 0, 1), moved(pieces[2], 1, 0), moved(pieces[3], 1, 1)
    shape = (field.shape[0], half, half, field.shape[-1])
    grid = lambda a: a.reshape(shape)
    upper = jnp.concatenate([grid(both), grid(lon_part)], 2)
    lower = jnp.concatenate([grid(lat_part), grid(pieces[0])], 2)
    return jnp.concatenate([upper, lower], 1)


def to_groups(blocks, place):
    out = [lax.dynamic_index_in_dim(blocks, place, 0, keepdims=False)]
    for k in range(1, PARTS):
        block = lax.dynamic_index_in_dim(blocks, (place + k) % PARTS, 0, keepdims=False)
        out.append(turned(block, 2 * k))
    return out


def cube_gather(parts):
    held = list(parts)
    for step in range(4):
        came = [swapped(held[p], "lat", DIRECTIONS[(p + step) % 4]) for p in range(PARTS)]
        if step == 3:
            return (held, came)
        held = [jnp.concatenate([held[p], came[p]], 0) for p in range(PARTS)]


def cube_sum(kept, sent):
    held = kept
    for step in range(3, -1, -1):
        came = [swapped(sent[p], "lat", DIRECTIONS[(p + step) % 4]) for p in range(PARTS)]
        total = [
            (held[p].astype(jnp.float32) + came[p].astype(jnp.float32)).astype(jnp.bfloat16)
            for p in range(PARTS)
        ]
        half = total[0].shape[0] // 2
        if step == 0:
            return total
        held = [t[:half] for t in total]
        sent = [t[half:] for t in total]


def body(
    tokens,
    cotangent,
    attention_in,
    attention_out,
    norm_attention,
    norm_expert,
    expert_up,
    expert_down,
    route_gain,
    assignment,
    slot_index,
):
    groups_n, lon_rows, lat_rows, features = tokens.shape
    lat_count = lax.axis_size("lat")
    lon_index = lax.axis_index("lon")
    lat_index = lax.axis_index("lat")
    place, core = lon_index // 2, lon_index % 2

    grad_out = (route_gain[..., None] * cotangent.astype(jnp.float32)).astype(jnp.bfloat16)
    named = jnp.transpose(assignment, (1, 2, 0)).astype(jnp.bfloat16)
    named = jnp.pad(named, ((0, 0), (0, 0), (0, features - groups_n)))
    everything = roll_in(jnp.concatenate([tokens, grad_out, named[None]], 0))
    rolled, grad_rows = everything[:groups_n], everything[groups_n : 2 * groups_n]
    named = everything[2 * groups_n][:, :groups_n].T
    named = jnp.pad(named[:, None, :], ((0, 0), (0, CHUNK - 1), (0, features - ROWS)))
    other_down = swapped(expert_down, "lon", 1)
    other_up = swapped(expert_up, "lon", 1)

    came = to_groups(jnp.concatenate([grad_rows, named], 1), place)
    shard = jnp.concatenate(
        [c[:ROWS] for c in came]
        + [c[ROWS : ROWS + 1] for c in came]
        + [jnp.zeros((SHARD - PARTS * (ROWS + 1), features), jnp.bfloat16)],
        0,
    )
    all_grads = lax.all_gather(shard, "lat", axis=0, tiled=True)

    zone_ids = ((jnp.arange(ROWS) // 16 % 2 == 1) & (lat_index == lat_count - 1)).astype(jnp.int32)
    produced, saved = attention_forward(
        rolled, zone_ids, attention_in, attention_out, norm_attention
    )
    middle = (rolled.astype(jnp.float32) + produced.astype(jnp.float32)).astype(jnp.bfloat16)
    normed = norm_rows(middle, norm_expert).astype(jnp.bfloat16)
    kept, late = cube_gather(to_groups(normed, place))

    cotangent = roll_in(cotangent)

    numbers = all_grads.reshape(lat_count, SHARD, features)[:, PARTS * ROWS : PARTS * (ROWS + 1), :ROWS]
    numbers = numbers.astype(jnp.int32) ^ (4 * core)
    masks = jnp.array([cube_masks(p) for p in range(PARTS)], jnp.int32)
    sources = lat_index ^ masks
    picked = (sources[..., None] == jnp.arange(lat_count)).astype(jnp.float32)
    numbers = jnp.einsum("pkj,jpr->pkr", picked, numbers.astype(jnp.float32)).astype(jnp.int32)
    offsets = sources * SHARD + ROWS * jnp.arange(PARTS)[:, None]

    halves = []
    for h, rows in ((0, kept), (1, late)):
        plan = routes(numbers[:, 8 * h : 8 * h + 8].reshape(TILES, TILE))
        spots, blocks, slots, slots_t = plan
        packed_grad, grad_hidden = grad_side(
            spots, blocks, offsets[:, 8 * h : 8 * h + 8].reshape(-1), all_grads, expert_down, other_down, slots
        )
        back, packed, hidden, grad_pre = expert_side(
            spots, blocks, rows, expert_up, other_up, grad_hidden, slots, slots_t
        )
        halves.append((back, blocks, packed, grad_pre, hidden, packed_grad))
    summed = cube_sum(halves[0][0], halves[1][0])
    weight_grads = ()
    for half in halves:
        weight_grads = weight_side(*half[1:], weight_grads)
    up_all, down_all = weight_grads
    grad_up = up_all[:4] + swapped(up_all[4:], "lon", 1)
    grad_down = down_all[:4] + swapped(down_all[4:], "lon", 1)

    returned = [summed[0]] + [turned(summed[k], -2 * k) for k in range(1, PARTS)]
    returned = jnp.roll(jnp.stack(returned), place, 0)
    grad_middle = cotangent.astype(jnp.float32) + norm_back(
        middle, norm_expert, returned.astype(jnp.float32)
    )
    grad_middle = grad_middle.astype(jnp.bfloat16)
    branch = attention_backward(
        saved, grad_middle, rolled, attention_in, attention_out, norm_attention
    )
    grad_tokens = (grad_middle.astype(jnp.float32) + branch.astype(jnp.float32)).astype(
        jnp.bfloat16
    )
    return (roll_out(grad_tokens), grad_up, grad_down)


def solution(mesh):
    return jax.shard_map(
        body,
        mesh=mesh,
        in_specs=(
            P(None, "lon", "lat", None),
            P(None, "lon", "lat", None),
            P(),
            P(),
            P(),
            P(),
            P("lon", None, "lat"),
            P("lon", "lat", None),
            P(None, "lon", "lat"),
            P(None, "lon", "lat"),
            P(None, "lon", "lat"),
        ),
        out_specs=(P(None, "lon", "lat", None), P("lon", None, "lat"), P("lon", "lat", None)),
        check_vma=False,
    )
```

```python
import functools
import math

import jax
import jax.numpy as jnp
from jax import lax
from jax.experimental import pallas as pl
from jax.experimental.pallas import tpu as pltpu
from jax.sharding import PartitionSpec as P

HS = 64
EPG = 8
WIN = 8
EPSILON = 1e-06
TANH_SCALE = math.sqrt(2.0 / math.pi)
CUBIC_COEF = 0.044715
MASKED = -1000000000.0

PARTS = 4
ROWS = 64
TILE = 256
CHUNK = 16
TILE_CHUNKS = 24
TILES = 8
BLOCK = 256
BLOCKS = 21
SPARE = (BLOCKS - 1) * (BLOCK // CHUNK)
STEPS = 2 * 19
AHEAD = 4
RING = 4
HEADS = 16
QUADS = 4
CELLS = 16
SLOTS = 9
SHARD = 2 * PARTS * ROWS
BUFFER = BLOCKS * BLOCK

ANY = pl.BlockSpec(memory_space=pl.ANY)
SMEM = pl.BlockSpec(memory_space=pltpu.SMEM)
VMEM = pl.BlockSpec(memory_space=pltpu.VMEM)


def swapped(block, axis, direction):
    return lax.ppermute(block, axis, [(i, i ^ direction) for i in range(lax.axis_size(axis))])


def turned(block, distance):
    devices = lax.axis_size("lon")
    return lax.ppermute(block, "lon", [(i, (i + distance) % devices) for i in range(devices)])


def moved(block, lon_step, lat_step):
    lons, lats = lax.axis_size("lon"), lax.axis_size("lat")
    route = [
        (i * lats + j, (i + lon_step) % lons * lats + (j + lat_step) % lats)
        for i in range(lons)
        for j in range(lats)
    ]
    return lax.ppermute(block, ("lon", "lat"), route)


def gelu_parts(preact):
    argument = TANH_SCALE * (preact + CUBIC_COEF * preact * preact * preact)
    tangent = jnp.tanh(argument)
    activated = 0.5 * preact * (1.0 + tangent)
    derivative = 0.5 * (1.0 + tangent) + 0.5 * preact * (1.0 - tangent * tangent) * TANH_SCALE * (
        1.0 + 3.0 * CUBIC_COEF * preact * preact
    )
    return (activated, derivative)


def norm_rows(field, gain_vec):
    values_f = field.astype(jnp.float32)
    factor = lax.rsqrt(jnp.mean(values_f * values_f, -1, keepdims=True) + EPSILON)
    return values_f * factor * gain_vec


def norm_back(field, gain_vec, grad_in):
    values_f = field.astype(jnp.float32)
    factor = lax.rsqrt(jnp.mean(values_f * values_f, -1, keepdims=True) + EPSILON)
    scaled_grad = grad_in * gain_vec
    inner_mean = jnp.mean(values_f * scaled_grad, -1, keepdims=True)
    return factor * scaled_grad - values_f * factor * factor * factor * inner_mean


def dot_f32(a, b, contract=((1,), (0,))):
    return lax.dot_general(a, b, (contract, ((), ())), preferred_element_type=jnp.float32)


def block_rows(index):
    return pl.ds(pl.multiple_of(index * BLOCK, BLOCK), BLOCK)


def chunk_rows(index):
    return pl.ds(pl.multiple_of(index * CHUNK, CHUNK), CHUNK)


def expert_kernel(place_ref, plan_ref, all_ref, up_own_ref, up_other_ref, down_own_ref, down_other_ref,
                  slots_row_ref, slots_col_ref,
                  back_ref, rows_out_ref, grads_out_ref, hidden_ref, gpre_ref,
                  raw, raw_grad, up, down, rows, grads, result, hidden, gpre, stage, back,
                  raw_sem, raw_grad_sem, weight_sem, rows_sem, grads_sem, hidden_sem, gpre_sem, back_sem):
    def tile(t):
        return pl.ds(t * TILE, TILE)

    def row_loads(n):
        slot = n % RING
        return [
            pltpu.make_async_copy(all_ref.at[pl.ds(n * SHARD + first, TILE)], target.at[slot], sem.at[slot])
            for first, target, sem in ((0, raw, raw_sem), (TILE, raw_grad, raw_grad_sem))
        ]

    def begin(n):
        if n < 2 * TILES:
            for load in row_loads(n):
                load.start()

    weight_loads = [
        pltpu.make_async_copy(up_own_ref, up.at[pl.ds(0, 4)], weight_sem.at[0]),
        pltpu.make_async_copy(up_other_ref, up.at[pl.ds(4, 4)], weight_sem.at[1]),
        pltpu.make_async_copy(down_own_ref, down.at[pl.ds(0, 4)], weight_sem.at[2]),
        pltpu.make_async_copy(down_other_ref, down.at[pl.ds(4, 4)], weight_sem.at[3]),
    ]
    for n in range(RING):
        begin(n)
    for load in weight_loads:
        load.start()

    def clear(b, carry):
        for buffer in (rows, grads):
            buffer[block_rows(b), :] = jnp.zeros((BLOCK, buffer.shape[1]), buffer.dtype)
        return carry

    result[SPARE * CHUNK : (SPARE + 1) * CHUNK, :] = jnp.zeros((CHUNK, result.shape[1]), result.dtype)
    backs = []
    for h in range(2):
        count = (plan_ref[h, BLOCKS] + 1) // 2 * 2

        def wide_stores(b):
            target = block_rows(h * BLOCKS + b)
            return [
                pltpu.make_async_copy(rows.at[block_rows(b)], rows_out_ref.at[target], rows_sem.at[b]),
                pltpu.make_async_copy(grads.at[block_rows(b)], grads_out_ref.at[target], grads_sem.at[b]),
            ]

        def narrow_stores(b):
            target = block_rows(h * BLOCKS + b)
            return [
                pltpu.make_async_copy(hidden.at[b % RING], hidden_ref.at[target], hidden_sem.at[b % RING]),
                pltpu.make_async_copy(gpre.at[b % RING], gpre_ref.at[target], gpre_sem.at[b % RING]),
            ]

        lax.fori_loop(0, count, clear, 0)
        spots = lax.broadcasted_iota(jnp.int32, (TILE_CHUNKS * CHUNK, TILE), 0)
        for n in range(h * TILES, (h + 1) * TILES):
            pick = (spots == slots_row_ref[n : n + 1, :]).astype(jnp.bfloat16)
            for load, source, buffer in zip(row_loads(n), (raw, raw_grad), (rows, grads)):
                load.wait()
                packed = dot_f32(pick, source[n % RING]).astype(jnp.bfloat16)
                for q in range(TILE_CHUNKS):
                    buffer[chunk_rows(place_ref[n, q]), :] = packed[q * CHUNK : (q + 1) * CHUNK]
            begin(n + RING)
        if h == 0:
            for load in weight_loads:
                load.wait()

        def step(pair, carry):
            both = (2 * pair, 2 * pair + 1)

            @pl.when(pair >= 2)
            def _():
                for b in both:
                    for store in narrow_stores(b - RING):
                        store.wait()

            preacts = [dot_f32(rows[block_rows(b), :], up[plan_ref[h, b]]) for b in both]
            grad_hiddens = [dot_f32(grads[block_rows(b), :], down[plan_ref[h, b]], ((1,), (1,))) for b in both]
            for b, preact, grad_hidden in zip(both, preacts, grad_hiddens):
                activated, derivative = gelu_parts(preact)
                hidden[b % RING] = activated.astype(jnp.bfloat16)
                grad_pre = (grad_hidden * derivative).astype(jnp.bfloat16)
                gpre[b % RING] = grad_pre
                result[block_rows(b), :] = dot_f32(grad_pre, up[plan_ref[h, b]], ((1,), (1,))).astype(jnp.bfloat16)
                for store in wide_stores(b) + narrow_stores(b):
                    store.start()
            return carry

        lax.fori_loop(0, count // 2, step, 0)

        spots = lax.broadcasted_iota(jnp.int32, (TILE, TILE_CHUNKS * CHUNK), 1)
        for t in range(TILES):
            n = h * TILES + t
            for q in range(TILE_CHUNKS):
                stage[q * CHUNK : (q + 1) * CHUNK, :] = result[chunk_rows(place_ref[n, q]), :]
            pick = (spots == slots_col_ref[:, n : n + 1]).astype(jnp.bfloat16)
            if n >= 2:
                backs[n - 2].wait()
            back[n % 2] = dot_f32(pick, stage[...]).astype(jnp.bfloat16)
            backs.append(pltpu.make_async_copy(back.at[n % 2], back_ref.at[tile(n)], back_sem.at[n % 2]))
            backs[n].start()

        def finish(b, carry):
            for store in wide_stores(b):
                store.wait()

            @pl.when(b >= count - RING)
            def _():
                for store in narrow_stores(b):
                    store.wait()

            return carry

        lax.fori_loop(0, count, finish, 0)
    for store in backs[-2:]:
        store.wait()


def expert_side(place, plan, rows, ups, downs, slots_row, slots_col):
    features, hidden_units = ups[0].shape[1:]
    wide = jax.ShapeDtypeStruct((2 * BUFFER, features), jnp.bfloat16)
    narrow = jax.ShapeDtypeStruct((2 * BUFFER, hidden_units), jnp.bfloat16)
    blocks_sem, ring_sem = pltpu.SemaphoreType.DMA((BLOCKS,)), pltpu.SemaphoreType.DMA((RING,))
    return pl.pallas_call(
        expert_kernel,
        out_shape=(jax.ShapeDtypeStruct((2 * TILES * TILE, features), jnp.bfloat16), wide, wide, narrow, narrow),
        in_specs=[SMEM] * 2 + [ANY] * 5 + [VMEM, VMEM],
        out_specs=(ANY,) * 5,
        scratch_shapes=[
            pltpu.VMEM((RING, TILE, features), jnp.bfloat16),
            pltpu.VMEM((RING, TILE, features), jnp.bfloat16),
            pltpu.VMEM((EPG, features, hidden_units), jnp.bfloat16),
            pltpu.VMEM((EPG, hidden_units, features), jnp.bfloat16),
            pltpu.VMEM((BUFFER, features), jnp.bfloat16),
            pltpu.VMEM((BUFFER, features), jnp.bfloat16),
            pltpu.VMEM((BUFFER, features), jnp.bfloat16),
            pltpu.VMEM((RING, BLOCK, hidden_units), jnp.bfloat16),
            pltpu.VMEM((RING, BLOCK, hidden_units), jnp.bfloat16),
            pltpu.VMEM((TILE_CHUNKS * CHUNK, features), jnp.bfloat16),
            pltpu.VMEM((2, TILE, features), jnp.bfloat16),
            ring_sem,
            ring_sem,
            ring_sem,
            blocks_sem,
            blocks_sem,
            ring_sem,
            ring_sem,
            pltpu.SemaphoreType.DMA((2,)),
        ],
        compiler_params=pltpu.CompilerParams(vmem_limit_bytes=52 * 2**20),
        cost_estimate=pl.CostEstimate(flops=30 * 10**9, bytes_accessed=64 * 2**20, transcendentals=2 * 10**6),
    )(place, plan, rows, *ups, *downs, slots_row, slots_col)


def weight_kernel(start_ref, block_ref, *refs):
    arrays, before = refs[:4], refs[4:-8]
    (up_ref, down_ref), buffers, (total, sems) = refs[-8:-6], refs[-6:-2], refs[-2:]
    expert = pl.program_id(0)
    count = start_ref[4]

    def loads(i):
        return [
            pltpu.make_async_copy(a.at[block_rows(block_ref[i])], buffer.at[i % AHEAD], sems.at[n, i % AHEAD])
            for n, (a, buffer) in enumerate(zip(arrays, buffers))
        ]

    def begin(i):
        @pl.when(i < count)
        def _():
            for load in loads(i):
                load.start()

    @pl.when(expert == 0)
    def _():
        for i in range(AHEAD - 1):
            begin(jnp.int32(i))

    total[...] = jnp.zeros_like(total)
    down_ref[...] = before[1][...] if before else jnp.zeros_like(down_ref)

    def step(i, carry):
        for load in loads(i):
            load.wait()
        begin(i + AHEAD - 1)
        rows, grads, hidden, gpre = [buffer[i % AHEAD] for buffer in buffers]
        total[...] += dot_f32(gpre, rows, ((0,), (0,)))
        down_ref[0] += dot_f32(hidden, grads, ((0,), (0,)))
        return carry

    lax.fori_loop(start_ref[expert], start_ref[expert + 1], step, 0)
    up_ref[0] = total[...].T + (before[0][0] if before else 0.0)


def weight_side(plan, arrays, before=()):
    features, hidden_units = arrays[0].shape[1], arrays[2].shape[1]
    up, down = (features, hidden_units), (hidden_units, features)
    outs = tuple(pl.BlockSpec((1, *shape), lambda e: (e, 0, 0)) for shape in (up, down))
    return pl.pallas_call(
        weight_kernel,
        out_shape=tuple(jax.ShapeDtypeStruct((4, *shape), jnp.float32) for shape in (up, down)),
        grid=(4,),
        in_specs=[SMEM] * 2 + [ANY] * 4 + list(outs[: len(before)]),
        out_specs=outs,
        scratch_shapes=[pltpu.VMEM((AHEAD, BLOCK, a.shape[1]), jnp.bfloat16) for a in arrays]
        + [pltpu.VMEM(down, jnp.float32), pltpu.SemaphoreType.DMA((4, AHEAD))],
        compiler_params=pltpu.CompilerParams(vmem_limit_bytes=52 * 2**20),
        cost_estimate=pl.CostEstimate(flops=4 * 10**9, bytes_accessed=25 * 2**20, transcendentals=0),
    )(*plan, *arrays, *before)


def weight_plan(counts, side):
    ahead = lambda v: jnp.cumsum(v) - v
    mine = slice(4 * side, 4 * side + 4)
    halves = [(ahead(c)[mine][None, :] + h * BLOCKS, c[mine][None, :]) for h, c in enumerate(counts)]
    totals = (halves[0][1] + halves[1][1])[0]
    starts = ahead(totals)
    step = jnp.arange(STEPS, dtype=jnp.int32)[:, None]
    inside = (step >= starts[None, :]) & (step < (starts + totals)[None, :])
    offset = step - starts[None, :]
    block = jnp.where(offset >= halves[0][1], halves[1][0] + offset - halves[0][1], halves[0][0] + offset)
    block = jnp.sum(jnp.where(inside, block, 0), 1)
    return (jnp.concatenate([starts, jnp.sum(totals)[None]]).astype(jnp.int32), block.astype(jnp.int32))


def routes(named):
    onehot = (named[..., None] == jnp.arange(EPG)).astype(jnp.bfloat16)
    earlier = jnp.tril(jnp.ones((TILE, TILE), jnp.bfloat16), -1)
    ranks = jnp.einsum("rs,tse->tre", earlier, onehot, preferred_element_type=jnp.float32)
    onehot_f = onehot.astype(jnp.float32)
    rank = jnp.sum(ranks * onehot_f, -1).astype(jnp.int32)
    counts = jnp.sum(onehot_f, 1).astype(jnp.int32)
    chunks = (counts + CHUNK - 1) // CHUNK

    def before(values, axis):
        return jnp.cumsum(values, axis) - values

    starts = before(chunks, 1)
    slots = CHUNK * jnp.sum(onehot_f * starts[:, None, :].astype(jnp.float32), -1).astype(jnp.int32) + rank
    per_block = BLOCK // CHUNK
    blocks = jnp.maximum((jnp.sum(chunks, 0) + per_block - 1) // per_block, 1)
    first_block = before(blocks, 0)
    places = first_block[None, :] * per_block + before(chunks, 0)
    index = jnp.arange(TILE_CHUNKS)[None, :, None]
    inside = (index >= starts[:, None, :]) & (index < (starts + chunks)[:, None, :])
    place = jnp.sum(jnp.where(inside, places[:, None, :] + index - starts[:, None, :] - SPARE, 0), -1) + SPARE
    number = jnp.arange(BLOCKS)[:, None]
    plan = jnp.sum((number >= first_block[None, :]).astype(jnp.int32), -1) - 1
    plan = jnp.concatenate([plan, jnp.sum(blocks)[None]]).astype(jnp.int32)
    return (place.astype(jnp.int32), plan, slots, slots.T, blocks)


def whole(shape):
    return pl.BlockSpec(shape, lambda i: (0,) * len(shape))


def pack_kernel(tokens_ref, cotangent_ref, gain_ref, named_ref, *refs):
    outs, later, scratch = refs[:QUADS], refs[QUADS : 2 * QUADS], refs[2 * QUADS]
    half = WIN // 2
    corners = ((half, half), (half, 0), (0, half), (0, 0))
    for g in range(tokens_ref.shape[0]):
        cotangent_f = cotangent_ref[g].astype(jnp.float32)
        fields = (tokens_ref[g].astype(jnp.float32), gain_ref[g] * cotangent_f, cotangent_f)
        for f, field in enumerate(fields):
            for q, (lon, lat) in enumerate(corners):
                for i in range(half):
                    scratch[f, q, half * i : half * (i + 1), :] = field[lon + i, lat : lat + half, :]
        for q in range(QUADS):
            outs[q][g] = scratch[0, q].astype(jnp.bfloat16)
            outs[q][4 + g] = scratch[1, q].astype(jnp.bfloat16)
            later[q][g] = scratch[2, q].astype(jnp.bfloat16)
    for q in range(QUADS):
        outs[q][SLOTS - 1] = named_ref[q]


def pack(tokens, cotangent, gain, named):
    features = tokens.shape[-1]
    piece = jax.ShapeDtypeStruct((SLOTS, CELLS, features), jnp.bfloat16)
    later = jax.ShapeDtypeStruct((4, CELLS, features), jnp.bfloat16)
    outs = pl.pallas_call(
        pack_kernel,
        out_shape=(piece,) * QUADS + (later,) * QUADS,
        in_specs=[VMEM] * 4,
        out_specs=(VMEM,) * (2 * QUADS),
        scratch_shapes=[pltpu.VMEM((3, QUADS, CELLS, features), jnp.float32)],
        compiler_params=pltpu.CompilerParams(vmem_limit_bytes=24 * 2**20),
    )(tokens, cotangent, gain, named)
    return (outs[:QUADS], outs[QUADS:])


def deal_kernel(where_ref, *refs):
    grads, named, outs = refs[:QUADS], refs[QUADS : 2 * QUADS], refs[2 * QUADS :]
    row = lax.broadcasted_iota(jnp.int32, (CHUNK, 1024), 0)
    for k in range(PARTS):
        group = (where_ref[0] + k) % PARTS
        numbers = jnp.zeros((CHUNK, 1024), jnp.float32)
        for q in range(QUADS):
            outs[k][q * CELLS : (q + 1) * CELLS, :] = grads[q][group]
            line = jnp.sum(jnp.where(row == group, named[q][0].astype(jnp.float32), 0.0), 0, keepdims=True)
            numbers += jnp.where(row == QUADS * k + q, line, 0.0)
        outs[k][ROWS : ROWS + CHUNK, :] = numbers.astype(jnp.bfloat16)


def deal(where, pieces):
    out = jax.ShapeDtypeStruct((ROWS + CHUNK, 1024), jnp.bfloat16)
    return pl.pallas_call(
        deal_kernel,
        out_shape=(out,) * PARTS,
        grid=(1,),
        in_specs=[SMEM]
        + [pl.BlockSpec((4, CELLS, 1024), lambda i: (1, 0, 0))] * QUADS
        + [pl.BlockSpec((1, CELLS, 1024), lambda i: (SLOTS - 1, 0, 0))] * QUADS,
        out_specs=(whole((ROWS + CHUNK, 1024)),) * PARTS,
        compiler_params=pltpu.CompilerParams(vmem_limit_bytes=52 * 2**20),
    )(where, *pieces, *pieces)


def shard_kernel(*refs):
    grads, rows, (out, numbers) = refs[:PARTS], refs[PARTS : 2 * PARTS], refs[2 * PARTS :]
    total = jnp.zeros((CHUNK, 1024), jnp.float32)
    for k in range(PARTS):
        out[k * ROWS : (k + 1) * ROWS, :] = rows[k][...]
        out[(PARTS + k) * ROWS : (PARTS + k + 1) * ROWS, :] = grads[k][:ROWS, :]
        total += grads[k][ROWS:, :].astype(jnp.float32)
    numbers[...] = total[:, :128]


def to_shard(grads, rows):
    return pl.pallas_call(
        shard_kernel,
        out_shape=(
            jax.ShapeDtypeStruct((SHARD, 1024), jnp.bfloat16),
            jax.ShapeDtypeStruct((CHUNK, 128), jnp.float32),
        ),
        in_specs=[VMEM] * (2 * PARTS),
        out_specs=(VMEM, VMEM),
    )(*grads, *rows)


def seen(where_ref, axis):
    cell = lax.broadcasted_iota(jnp.int32, (4 * ROWS, 4 * ROWS), axis)
    return cell // ROWS * 2 + cell // CELLS % 2 * where_ref[1]


def softmax_of(projected, visible, h):
    queries = projected[:, h * HS : (h + 1) * HS]
    keyset = projected[:, (HEADS + h) * HS : (HEADS + h + 1) * HS]
    scores = dot_f32(queries, keyset, ((1,), (1,))) * HS ** (-0.5)
    scores = jnp.where(visible[...] > 0, scores, MASKED)
    weights_exp = jnp.exp(scores - jnp.max(scores, -1, keepdims=True))
    return (queries, keyset, weights_exp / jnp.sum(weights_exp, -1, keepdims=True))


def forward_kernel(where_ref, p0, p1, p2, p3, gain1_ref, gain2_ref, win_ref, wout_ref,
                   rolled, projected, middle, n0, n1, n2, n3,
                   win, wout, normed, attended, visible, sems):
    loads = [
        pltpu.make_async_copy(win_ref.at[:, pl.ds(1024 * c, 1024)], win.at[c], sems.at[c]) for c in range(3)
    ] + [pltpu.make_async_copy(wout_ref, wout, sems.at[3])]
    for load in loads:
        load.start()
    visible[...] = (seen(where_ref, 0) == seen(where_ref, 1)).astype(jnp.float32)
    for g in range(4):
        for q, piece in enumerate((p0, p1, p2, p3)):
            rolled[g * ROWS + q * CELLS : g * ROWS + (q + 1) * CELLS, :] = piece[g]
        window = slice(g * ROWS, (g + 1) * ROWS)
        normed[window, :] = norm_rows(rolled[window, :], gain1_ref[...]).astype(jnp.bfloat16)
    for c in range(3):
        loads[c].wait()
        projected[:, c * 1024 : (c + 1) * 1024] = dot_f32(normed[...], win[c]).astype(jnp.bfloat16)
    for pair in range(HEADS // 2):
        both = []
        for h in (2 * pair, 2 * pair + 1):
            probs = softmax_of(projected, visible, h)[2]
            values = projected[:, (2 * HEADS + h) * HS : (2 * HEADS + h + 1) * HS]
            both.append(dot_f32(probs.astype(jnp.bfloat16), values))
        attended[:, pair * 2 * HS : (pair + 1) * 2 * HS] = jnp.concatenate(both, 1).astype(jnp.bfloat16)
    loads[3].wait()
    produced = dot_f32(attended[...], wout[...]).astype(jnp.bfloat16)
    for g in range(4):
        window = slice(g * ROWS, (g + 1) * ROWS)
        total = rolled[window, :].astype(jnp.float32) + produced[window, :].astype(jnp.float32)
        middle[window, :] = total.astype(jnp.bfloat16)
        normed[window, :] = norm_rows(middle[window, :], gain2_ref[...]).astype(jnp.bfloat16)
    for k, out in enumerate((n0, n1, n2, n3)):
        group = (where_ref[0] + k) % PARTS
        out[...] = normed[pl.ds(pl.multiple_of(group * ROWS, ROWS), ROWS), :]


def attention_forward(where, pieces, gain1, gain2, weight_in, weight_out):
    rows = 4 * ROWS
    field = jax.ShapeDtypeStruct((rows, 1024), jnp.bfloat16)
    part = jax.ShapeDtypeStruct((ROWS, 1024), jnp.bfloat16)
    return pl.pallas_call(
        forward_kernel,
        out_shape=(field, jax.ShapeDtypeStruct((rows, 3072), jnp.bfloat16), field) + (part,) * PARTS,
        grid=(1,),
        in_specs=[SMEM]
        + [whole((4, CELLS, 1024))] * QUADS
        + [whole((1, 1024))] * 2
        + [ANY, ANY],
        out_specs=(whole((rows, 1024)), whole((rows, 3072)), whole((rows, 1024))) + (whole((ROWS, 1024)),) * PARTS,
        scratch_shapes=[
            pltpu.VMEM((3, 1024, 1024), jnp.bfloat16),
            pltpu.VMEM((1024, 1024), jnp.bfloat16),
            pltpu.VMEM((rows, 1024), jnp.bfloat16),
            pltpu.VMEM((rows, 1024), jnp.bfloat16),
            pltpu.VMEM((rows, rows), jnp.float32),
            pltpu.SemaphoreType.DMA((4,)),
        ],
        compiler_params=pltpu.CompilerParams(vmem_limit_bytes=52 * 2**20),
        cost_estimate=pl.CostEstimate(flops=4 * 10**9, bytes_accessed=14 * 2**20, transcendentals=2**20),
    )(where, *pieces, gain1, gain2, weight_in, weight_out)


def backward_kernel(where_ref, r0, r1, r2, r3, c0, c1, c2, c3, middle, rolled, projected, gain1_ref, gain2_ref,
                    win_ref, wout_ref, o0, o1, o2, o3,
                    win, wout, arrived, grad_middle, grad_att, grad_proj, visible, sems):
    loads = [
        pltpu.make_async_copy(win_ref.at[:, pl.ds(1024 * c, 1024)], win.at[c], sems.at[c]) for c in range(3)
    ] + [pltpu.make_async_copy(wout_ref, wout, sems.at[3])]
    for load in loads[::-1]:
        load.start()
    visible[...] = (seen(where_ref, 0) == seen(where_ref, 1)).astype(jnp.float32)
    for k, part in enumerate((r0, r1, r2, r3)):
        group = (where_ref[0] + k) % PARTS
        arrived[pl.ds(pl.multiple_of(group * ROWS, ROWS), ROWS), :] = part[...]
    for g in range(4):
        window = slice(g * ROWS, (g + 1) * ROWS)
        cotangent = jnp.concatenate([c[g] for c in (c0, c1, c2, c3)], 0).astype(jnp.float32)
        back = norm_back(middle[window, :], gain2_ref[...], arrived[window, :].astype(jnp.float32))
        grad_middle[window, :] = (cotangent + back).astype(jnp.bfloat16)
    loads[3].wait()
    grad_att[...] = dot_f32(grad_middle[...], wout[...], ((1,), (1,))).astype(jnp.bfloat16)
    for pair in range(HEADS // 2):
        grads = ([], [], [])
        for h in (2 * pair, 2 * pair + 1):
            queries, keyset, probs = softmax_of(projected, visible, h)
            values = projected[:, (2 * HEADS + h) * HS : (2 * HEADS + h + 1) * HS]
            grad_head = grad_att[:, h * HS : (h + 1) * HS]
            grad_probs = dot_f32(grad_head, values, ((1,), (1,)))
            grad_scores = probs * (grad_probs - jnp.sum(probs * grad_probs, -1, keepdims=True))
            scaled = (grad_scores * HS ** (-0.5)).astype(jnp.bfloat16)
            grads[0].append(dot_f32(scaled, keyset))
            grads[1].append(dot_f32(scaled, queries, ((0,), (0,))))
            grads[2].append(dot_f32(probs.astype(jnp.bfloat16), grad_head, ((0,), (0,))))
        for c in range(3):
            start = (c * HEADS + 2 * pair) * HS
            grad_proj[:, start : start + 2 * HS] = jnp.concatenate(grads[c], 1).astype(jnp.bfloat16)
    for load in loads[:3]:
        load.wait()
    grad_norm = sum(
        dot_f32(grad_proj[:, c * 1024 : (c + 1) * 1024], win[c], ((1,), (1,))) for c in range(3)
    )
    for g in range(4):
        window = slice(g * ROWS, (g + 1) * ROWS)
        branch = norm_back(rolled[window, :], gain1_ref[...], grad_norm[window, :]).astype(jnp.bfloat16)
        total = grad_middle[window, :].astype(jnp.float32) + branch.astype(jnp.float32)
        for q, out in enumerate((o0, o1, o2, o3)):
            out[g] = total[q * CELLS : (q + 1) * CELLS, :].astype(jnp.bfloat16)


def attention_backward(where, returned, pieces, middle, rolled, projected, gain1, gain2, weight_in, weight_out):
    rows = 4 * ROWS
    piece = jax.ShapeDtypeStruct((4, CELLS, 1024), jnp.bfloat16)
    return pl.pallas_call(
        backward_kernel,
        out_shape=(piece,) * QUADS,
        grid=(1,),
        in_specs=[SMEM]
        + [whole((ROWS, 1024))] * PARTS
        + [whole((4, CELLS, 1024))] * QUADS
        + [whole((rows, 1024))] * 2
        + [whole((rows, 3072))]
        + [whole((1, 1024))] * 2
        + [ANY, ANY],
        out_specs=(whole((4, CELLS, 1024)),) * QUADS,
        scratch_shapes=[
            pltpu.VMEM((3, 1024, 1024), jnp.bfloat16),
            pltpu.VMEM((1024, 1024), jnp.bfloat16),
            pltpu.VMEM((rows, 1024), jnp.bfloat16),
            pltpu.VMEM((rows, 1024), jnp.bfloat16),
            pltpu.VMEM((rows, 1024), jnp.bfloat16),
            pltpu.VMEM((rows, 3072), jnp.bfloat16),
            pltpu.VMEM((rows, rows), jnp.float32),
            pltpu.SemaphoreType.DMA((4,)),
        ],
        compiler_params=pltpu.CompilerParams(vmem_limit_bytes=52 * 2**20),
        cost_estimate=pl.CostEstimate(flops=6 * 10**9, bytes_accessed=14 * 2**20, transcendentals=2**20),
    )(where, *returned, *pieces, middle, rolled, projected, gain1, gain2, weight_in, weight_out)


def roll_out(pieces):
    half = WIN // 2
    stays, lat_part, lon_part, both = pieces
    shape = (pieces[0].shape[0], half, half, pieces[0].shape[-1])
    grid = lambda a: a.reshape(shape)
    upper = jnp.concatenate([grid(both), grid(lon_part)], 2)
    lower = jnp.concatenate([grid(lat_part), grid(stays)], 2)
    return jnp.concatenate([upper, lower], 1)


def spread(blocks):
    return [blocks[0]] + [turned(blocks[k], 2 * k) for k in range(1, PARTS)]


def body(
    tokens,
    cotangent,
    attention_in,
    attention_out,
    norm_attention,
    norm_expert,
    expert_up,
    expert_down,
    route_gain,
    assignment,
    slot_index,
):
    groups_n, lon_rows, lat_rows, features = tokens.shape
    lat_count = lax.axis_size("lat")
    lon_index = lax.axis_index("lon")
    lat_index = lax.axis_index("lat")
    place, core = lon_index // 2, lon_index % 2
    where = jnp.stack([place, (lat_index == lat_count - 1).astype(place.dtype)]).astype(jnp.int32)
    gain1, gain2 = norm_attention[None, :], norm_expert[None, :]

    half = WIN // 2
    named = assignment.reshape(groups_n, 2, half, 2, half).transpose(1, 3, 0, 2, 4)[::-1, ::-1]
    named = named.reshape(QUADS, groups_n, CELLS).astype(jnp.bfloat16)
    named = jnp.pad(named, ((0, 0), (0, CHUNK - groups_n), (0, features - CELLS)))
    def roll_in(parts):
        return (parts[0], moved(parts[1], 0, -1), moved(parts[2], -1, 0), moved(parts[3], -1, -1))

    first, later = pack(tokens, cotangent, route_gain[..., None], named)
    first = roll_in(first)
    dealt = deal(where, first)
    first, dealt = lax.optimization_barrier((first, dealt))
    grads = spread(dealt)

    rolled, projected, middle, *normed = attention_forward(
        where, first, gain1, gain2, attention_in, attention_out
    )
    shard, numbers = to_shard(grads, spread(normed))
    rows = lax.all_gather(shard, "lat", axis=0, tiled=True)

    numbers, expert_down, expert_up, later = lax.optimization_barrier((numbers, expert_down, expert_up, later))
    ups, downs = (expert_up, swapped(expert_up, "lon", 1)), (expert_down, swapped(expert_down, "lon", 1))
    later = roll_in(later)

    numbers, later = lax.optimization_barrier((numbers, later))
    numbers = lax.all_gather(numbers.astype(jnp.int32), "lat", axis=0)
    numbers = numbers[:, :, :CELLS].reshape(lat_count, PARTS * ROWS) ^ (4 * core)
    places, plans, slots, slots_t, counts = zip(*[routes(numbers[TILES * h : TILES * (h + 1)]) for h in range(2)])

    back, *arrays = expert_side(
        jnp.concatenate(places, 0), jnp.stack(plans), rows, ups, downs,
        jnp.concatenate(slots, 0), jnp.concatenate(slots_t, 1),
    )
    summed = lax.psum_scatter(back, "lat", scatter_dimension=0, tiled=True)
    came = [swapped(a, "lon", 1) for a in weight_side(weight_plan(counts, 1), arrays)]
    grad_up, grad_down = weight_side(weight_plan(counts, 0), arrays, came)

    summed, grad_up, grad_down = lax.optimization_barrier((summed, grad_up, grad_down))
    summed = [summed[k * ROWS : (k + 1) * ROWS] for k in range(PARTS)]
    returned = [summed[0]] + [turned(summed[k], -2 * k) for k in range(1, PARTS)]
    out = attention_backward(
        where, returned, later, middle, rolled, projected, gain1, gain2, attention_in, attention_out
    )
    came = [moved(out[1], 0, 1), moved(out[2], 1, 0), moved(out[3], 1, 1)]
    return (roll_out([out[0], *came]), grad_up, grad_down)


def solution(mesh):
    return jax.shard_map(
        body,
        mesh=mesh,
        in_specs=(
            P(None, "lon", "lat", None),
            P(None, "lon", "lat", None),
            P(),
            P(),
            P(),
            P(),
            P("lon", None, "lat"),
            P("lon", "lat", None),
            P(None, "lon", "lat"),
            P(None, "lon", "lat"),
            P(None, "lon", "lat"),
        ),
        out_specs=(P(None, "lon", "lat", None), P("lon", None, "lat"), P("lon", "lat", None)),
        check_vma=False,
    )
```

```python
import functools
import math

import jax
import jax.numpy as jnp
from jax import lax
from jax.experimental import pallas as pl
from jax.experimental.pallas import tpu as pltpu
from jax.sharding import PartitionSpec as P

HS = 64
EPG = 8
WIN = 8
EPSILON = 1e-06
TANH_SCALE = math.sqrt(2.0 / math.pi)
CUBIC_COEF = 0.044715
MASKED = -1000000000.0

PARTS = 4
ROWS = 64
TILE = 256
CHUNK = 16
TILE_CHUNKS = 24
TILES = 8
BLOCK = 256
BLOCKS = 21
SPARE = (BLOCKS - 1) * (BLOCK // CHUNK)
STEPS = 2 * 19
AHEAD = 4
RING = 4
HEADS = 16
QUADS = 4
CELLS = 16
SLOTS = 9
SHARD = 2 * PARTS * ROWS
BUFFER = BLOCKS * BLOCK

ANY = pl.BlockSpec(memory_space=pl.ANY)
SMEM = pl.BlockSpec(memory_space=pltpu.SMEM)
VMEM = pl.BlockSpec(memory_space=pltpu.VMEM)


def swapped(block, axis, direction):
    return lax.ppermute(block, axis, [(i, i ^ direction) for i in range(lax.axis_size(axis))])


def turned(block, distance):
    devices = lax.axis_size("lon")
    return lax.ppermute(block, "lon", [(i, (i + distance) % devices) for i in range(devices)])


def moved(block, lon_step, lat_step):
    lons, lats = lax.axis_size("lon"), lax.axis_size("lat")
    route = [
        (i * lats + j, (i + lon_step) % lons * lats + (j + lat_step) % lats)
        for i in range(lons)
        for j in range(lats)
    ]
    return lax.ppermute(block, ("lon", "lat"), route)


def gelu_parts(preact):
    argument = TANH_SCALE * (preact + CUBIC_COEF * preact * preact * preact)
    tangent = jnp.tanh(argument)
    activated = 0.5 * preact * (1.0 + tangent)
    derivative = 0.5 * (1.0 + tangent) + 0.5 * preact * (1.0 - tangent * tangent) * TANH_SCALE * (
        1.0 + 3.0 * CUBIC_COEF * preact * preact
    )
    return (activated, derivative)


def norm_rows(field, gain_vec):
    values_f = field.astype(jnp.float32)
    factor = lax.rsqrt(jnp.mean(values_f * values_f, -1, keepdims=True) + EPSILON)
    return values_f * factor * gain_vec


def norm_back(field, gain_vec, grad_in):
    values_f = field.astype(jnp.float32)
    factor = lax.rsqrt(jnp.mean(values_f * values_f, -1, keepdims=True) + EPSILON)
    scaled_grad = grad_in * gain_vec
    inner_mean = jnp.mean(values_f * scaled_grad, -1, keepdims=True)
    return factor * scaled_grad - values_f * factor * factor * factor * inner_mean


def dot_f32(a, b, contract=((1,), (0,))):
    return lax.dot_general(a, b, (contract, ((), ())), preferred_element_type=jnp.float32)


def block_rows(index):
    return pl.ds(pl.multiple_of(index * BLOCK, BLOCK), BLOCK)


def chunk_rows(index):
    return pl.ds(pl.multiple_of(index * CHUNK, CHUNK), CHUNK)


def expert_kernel(place_ref, plan_ref, all_ref, up_own_ref, up_other_ref, down_own_ref, down_other_ref,
                  slots_row_ref, slots_col_ref,
                  back_ref, rows_out_ref, grads_out_ref, hidden_ref, gpre_ref,
                  raw, raw_grad, up, down, rows, grads, result, hidden, gpre, stage, back,
                  raw_sem, raw_grad_sem, weight_sem, rows_sem, grads_sem, hidden_sem, gpre_sem, back_sem):
    def tile(t):
        return pl.ds(t * TILE, TILE)

    def row_loads(n):
        slot = n % RING
        return [
            pltpu.make_async_copy(all_ref.at[pl.ds(n * SHARD + first, TILE)], target.at[slot], sem.at[slot])
            for first, target, sem in ((0, raw, raw_sem), (TILE, raw_grad, raw_grad_sem))
        ]

    def begin(n):
        if n < 2 * TILES:
            for load in row_loads(n):
                load.start()

    weight_loads = [
        pltpu.make_async_copy(up_own_ref, up.at[pl.ds(0, 4)], weight_sem.at[0]),
        pltpu.make_async_copy(up_other_ref, up.at[pl.ds(4, 4)], weight_sem.at[1]),
        pltpu.make_async_copy(down_own_ref, down.at[pl.ds(0, 4)], weight_sem.at[2]),
        pltpu.make_async_copy(down_other_ref, down.at[pl.ds(4, 4)], weight_sem.at[3]),
    ]
    for n in range(RING):
        begin(n)
    for load in weight_loads:
        load.start()

    def clear(b, carry):
        for buffer in (rows, grads):
            buffer[block_rows(b), :] = jnp.zeros((BLOCK, buffer.shape[1]), buffer.dtype)
        return carry

    result[SPARE * CHUNK : (SPARE + 1) * CHUNK, :] = jnp.zeros((CHUNK, result.shape[1]), result.dtype)
    backs = []
    for h in range(2):
        count = (plan_ref[h, BLOCKS] + 1) // 2 * 2

        def wide_stores(b):
            target = block_rows(h * BLOCKS + b)
            return [
                pltpu.make_async_copy(rows.at[block_rows(b)], rows_out_ref.at[target], rows_sem.at[b]),
                pltpu.make_async_copy(grads.at[block_rows(b)], grads_out_ref.at[target], grads_sem.at[b]),
            ]

        def narrow_stores(b):
            target = block_rows(h * BLOCKS + b)
            return [
                pltpu.make_async_copy(hidden.at[b % RING], hidden_ref.at[target], hidden_sem.at[b % RING]),
                pltpu.make_async_copy(gpre.at[b % RING], gpre_ref.at[target], gpre_sem.at[b % RING]),
            ]

        lax.fori_loop(0, count, clear, 0)
        spots = lax.broadcasted_iota(jnp.int32, (TILE_CHUNKS * CHUNK, TILE), 0)
        for n in range(h * TILES, (h + 1) * TILES):
            pick = (spots == slots_row_ref[n : n + 1, :]).astype(jnp.bfloat16)
            for load, source, buffer in zip(row_loads(n), (raw, raw_grad), (rows, grads)):
                load.wait()
                packed = dot_f32(pick, source[n % RING]).astype(jnp.bfloat16)
                for q in range(TILE_CHUNKS):
                    buffer[chunk_rows(place_ref[n, q]), :] = packed[q * CHUNK : (q + 1) * CHUNK]
            begin(n + RING)
        if h == 0:
            for load in weight_loads:
                load.wait()

        def step(pair, carry):
            both = (2 * pair, 2 * pair + 1)

            @pl.when(pair >= 2)
            def _():
                for b in both:
                    for store in narrow_stores(b - RING):
                        store.wait()

            preacts = [dot_f32(rows[block_rows(b), :], up[plan_ref[h, b]]) for b in both]
            grad_hiddens = [dot_f32(grads[block_rows(b), :], down[plan_ref[h, b]], ((1,), (1,))) for b in both]
            for b, preact, grad_hidden in zip(both, preacts, grad_hiddens):
                activated, derivative = gelu_parts(preact)
                hidden[b % RING] = activated.astype(jnp.bfloat16)
                grad_pre = (grad_hidden * derivative).astype(jnp.bfloat16)
                gpre[b % RING] = grad_pre
                result[block_rows(b), :] = dot_f32(grad_pre, up[plan_ref[h, b]], ((1,), (1,))).astype(jnp.bfloat16)
                for store in wide_stores(b) + narrow_stores(b):
                    store.start()
            return carry

        lax.fori_loop(0, count // 2, step, 0)

        spots = lax.broadcasted_iota(jnp.int32, (TILE, TILE_CHUNKS * CHUNK), 1)
        for t in range(TILES):
            n = h * TILES + t
            for q in range(TILE_CHUNKS):
                stage[q * CHUNK : (q + 1) * CHUNK, :] = result[chunk_rows(place_ref[n, q]), :]
            pick = (spots == slots_col_ref[:, n : n + 1]).astype(jnp.bfloat16)
            if n >= 2:
                backs[n - 2].wait()
            back[n % 2] = dot_f32(pick, stage[...]).astype(jnp.bfloat16)
            backs.append(pltpu.make_async_copy(back.at[n % 2], back_ref.at[tile(n)], back_sem.at[n % 2]))
            backs[n].start()

        def finish(b, carry):
            for store in wide_stores(b):
                store.wait()

            @pl.when(b >= count - RING)
            def _():
                for store in narrow_stores(b):
                    store.wait()

            return carry

        lax.fori_loop(0, count, finish, 0)
    for store in backs[-2:]:
        store.wait()


def expert_side(place, plan, rows, ups, downs, slots_row, slots_col):
    features, hidden_units = ups[0].shape[1:]
    wide = jax.ShapeDtypeStruct((2 * BUFFER, features), jnp.bfloat16)
    narrow = jax.ShapeDtypeStruct((2 * BUFFER, hidden_units), jnp.bfloat16)
    blocks_sem, ring_sem = pltpu.SemaphoreType.DMA((BLOCKS,)), pltpu.SemaphoreType.DMA((RING,))
    return pl.pallas_call(
        expert_kernel,
        out_shape=(jax.ShapeDtypeStruct((2 * TILES * TILE, features), jnp.bfloat16), wide, wide, narrow, narrow),
        in_specs=[SMEM] * 2 + [ANY] * 5 + [VMEM, VMEM],
        out_specs=(ANY,) * 5,
        scratch_shapes=[
            pltpu.VMEM((RING, TILE, features), jnp.bfloat16),
            pltpu.VMEM((RING, TILE, features), jnp.bfloat16),
            pltpu.VMEM((EPG, features, hidden_units), jnp.bfloat16),
            pltpu.VMEM((EPG, hidden_units, features), jnp.bfloat16),
            pltpu.VMEM((BUFFER, features), jnp.bfloat16),
            pltpu.VMEM((BUFFER, features), jnp.bfloat16),
            pltpu.VMEM((BUFFER, features), jnp.bfloat16),
            pltpu.VMEM((RING, BLOCK, hidden_units), jnp.bfloat16),
            pltpu.VMEM((RING, BLOCK, hidden_units), jnp.bfloat16),
            pltpu.VMEM((TILE_CHUNKS * CHUNK, features), jnp.bfloat16),
            pltpu.VMEM((2, TILE, features), jnp.bfloat16),
            ring_sem,
            ring_sem,
            ring_sem,
            blocks_sem,
            blocks_sem,
            ring_sem,
            ring_sem,
            pltpu.SemaphoreType.DMA((2,)),
        ],
        compiler_params=pltpu.CompilerParams(vmem_limit_bytes=52 * 2**20),
        cost_estimate=pl.CostEstimate(flops=30 * 10**9, bytes_accessed=64 * 2**20, transcendentals=2 * 10**6),
    )(place, plan, rows, *ups, *downs, slots_row, slots_col)


def weight_kernel(start_ref, block_ref, *refs):
    arrays, before = refs[:4], refs[4:-8]
    (up_ref, down_ref), buffers, (total, sems) = refs[-8:-6], refs[-6:-2], refs[-2:]
    expert = pl.program_id(0)
    count = start_ref[4]

    def loads(i):
        return [
            pltpu.make_async_copy(a.at[block_rows(block_ref[i])], buffer.at[i % AHEAD], sems.at[n, i % AHEAD])
            for n, (a, buffer) in enumerate(zip(arrays, buffers))
        ]

    def begin(i):
        @pl.when(i < count)
        def _():
            for load in loads(i):
                load.start()

    @pl.when(expert == 0)
    def _():
        for i in range(AHEAD - 1):
            begin(jnp.int32(i))

    total[...] = jnp.zeros_like(total)
    down_ref[...] = before[1][...] if before else jnp.zeros_like(down_ref)

    def step(i, carry):
        for load in loads(i):
            load.wait()
        begin(i + AHEAD - 1)
        rows, grads, hidden, gpre = [buffer[i % AHEAD] for buffer in buffers]
        total[...] += dot_f32(gpre, rows, ((0,), (0,)))
        down_ref[0] += dot_f32(hidden, grads, ((0,), (0,)))
        return carry

    lax.fori_loop(start_ref[expert], start_ref[expert + 1], step, 0)
    up_ref[0] = total[...].T + (before[0][0] if before else 0.0)


def weight_side(plan, arrays, before=()):
    features, hidden_units = arrays[0].shape[1], arrays[2].shape[1]
    up, down = (features, hidden_units), (hidden_units, features)
    outs = tuple(pl.BlockSpec((1, *shape), lambda e: (e, 0, 0)) for shape in (up, down))
    return pl.pallas_call(
        weight_kernel,
        out_shape=tuple(jax.ShapeDtypeStruct((4, *shape), jnp.float32) for shape in (up, down)),
        grid=(4,),
        in_specs=[SMEM] * 2 + [ANY] * 4 + list(outs[: len(before)]),
        out_specs=outs,
        scratch_shapes=[pltpu.VMEM((AHEAD, BLOCK, a.shape[1]), jnp.bfloat16) for a in arrays]
        + [pltpu.VMEM(down, jnp.float32), pltpu.SemaphoreType.DMA((4, AHEAD))],
        compiler_params=pltpu.CompilerParams(vmem_limit_bytes=52 * 2**20),
        cost_estimate=pl.CostEstimate(flops=4 * 10**9, bytes_accessed=25 * 2**20, transcendentals=0),
    )(*plan, *arrays, *before)


def weight_plan(counts, side):
    ahead = lambda v: jnp.cumsum(v) - v
    mine = slice(4 * side, 4 * side + 4)
    halves = [(ahead(c)[mine][None, :] + h * BLOCKS, c[mine][None, :]) for h, c in enumerate(counts)]
    totals = (halves[0][1] + halves[1][1])[0]
    starts = ahead(totals)
    step = jnp.arange(STEPS, dtype=jnp.int32)[:, None]
    inside = (step >= starts[None, :]) & (step < (starts + totals)[None, :])
    offset = step - starts[None, :]
    block = jnp.where(offset >= halves[0][1], halves[1][0] + offset - halves[0][1], halves[0][0] + offset)
    block = jnp.sum(jnp.where(inside, block, 0), 1)
    return (jnp.concatenate([starts, jnp.sum(totals)[None]]).astype(jnp.int32), block.astype(jnp.int32))


def routes(named):
    onehot = (named[..., None] == jnp.arange(EPG)).astype(jnp.bfloat16)
    earlier = jnp.tril(jnp.ones((TILE, TILE), jnp.bfloat16), -1)
    ranks = jnp.einsum("rs,tse->tre", earlier, onehot, preferred_element_type=jnp.float32)
    onehot_f = onehot.astype(jnp.float32)
    rank = jnp.sum(ranks * onehot_f, -1).astype(jnp.int32)
    counts = jnp.sum(onehot_f, 1).astype(jnp.int32)
    chunks = (counts + CHUNK - 1) // CHUNK

    def before(values, axis):
        return jnp.cumsum(values, axis) - values

    starts = before(chunks, 1)
    slots = CHUNK * jnp.sum(onehot_f * starts[:, None, :].astype(jnp.float32), -1).astype(jnp.int32) + rank
    per_block = BLOCK // CHUNK
    blocks = jnp.maximum((jnp.sum(chunks, 0) + per_block - 1) // per_block, 1)
    first_block = before(blocks, 0)
    places = first_block[None, :] * per_block + before(chunks, 0)
    index = jnp.arange(TILE_CHUNKS)[None, :, None]
    inside = (index >= starts[:, None, :]) & (index < (starts + chunks)[:, None, :])
    place = jnp.sum(jnp.where(inside, places[:, None, :] + index - starts[:, None, :] - SPARE, 0), -1) + SPARE
    number = jnp.arange(BLOCKS)[:, None]
    plan = jnp.sum((number >= first_block[None, :]).astype(jnp.int32), -1) - 1
    plan = jnp.concatenate([plan, jnp.sum(blocks)[None]]).astype(jnp.int32)
    return (place.astype(jnp.int32), plan, slots, slots.T, blocks)


def whole(shape):
    return pl.BlockSpec(shape, lambda i: (0,) * len(shape))


def pack_kernel(tokens_ref, cotangent_ref, gain_ref, named_ref, *refs):
    outs, later, scratch = refs[:QUADS], refs[QUADS : 2 * QUADS], refs[2 * QUADS]
    half = WIN // 2
    corners = ((half, half), (half, 0), (0, half), (0, 0))
    for g in range(tokens_ref.shape[0]):
        cotangent_f = cotangent_ref[g].astype(jnp.float32)
        fields = (tokens_ref[g].astype(jnp.float32), gain_ref[g] * cotangent_f, cotangent_f)
        for f, field in enumerate(fields):
            for q, (lon, lat) in enumerate(corners):
                for i in range(half):
                    scratch[f, q, half * i : half * (i + 1), :] = field[lon + i, lat : lat + half, :]
        for q in range(QUADS):
            outs[q][g] = scratch[0, q].astype(jnp.bfloat16)
            outs[q][4 + g] = scratch[1, q].astype(jnp.bfloat16)
            later[q][g] = scratch[2, q].astype(jnp.bfloat16)
    for q in range(QUADS):
        outs[q][SLOTS - 1] = named_ref[q]


def pack(tokens, cotangent, gain, named):
    features = tokens.shape[-1]
    piece = jax.ShapeDtypeStruct((SLOTS, CELLS, features), jnp.bfloat16)
    later = jax.ShapeDtypeStruct((4, CELLS, features), jnp.bfloat16)
    outs = pl.pallas_call(
        pack_kernel,
        out_shape=(piece,) * QUADS + (later,) * QUADS,
        in_specs=[VMEM] * 4,
        out_specs=(VMEM,) * (2 * QUADS),
        scratch_shapes=[pltpu.VMEM((3, QUADS, CELLS, features), jnp.float32)],
        compiler_params=pltpu.CompilerParams(vmem_limit_bytes=24 * 2**20),
    )(tokens, cotangent, gain, named)
    return (outs[:QUADS], outs[QUADS:])


def deal_kernel(where_ref, *refs):
    grads, named, outs = refs[:QUADS], refs[QUADS : 2 * QUADS], refs[2 * QUADS :]
    row = lax.broadcasted_iota(jnp.int32, (CHUNK, 1024), 0)
    for k in range(PARTS):
        group = (where_ref[0] + k) % PARTS
        numbers = jnp.zeros((CHUNK, 1024), jnp.float32)
        for q in range(QUADS):
            outs[k][q * CELLS : (q + 1) * CELLS, :] = grads[q][group]
            line = jnp.sum(jnp.where(row == group, named[q][0].astype(jnp.float32), 0.0), 0, keepdims=True)
            numbers += jnp.where(row == QUADS * k + q, line, 0.0)
        outs[k][ROWS : ROWS + CHUNK, :] = numbers.astype(jnp.bfloat16)


def deal(where, pieces):
    out = jax.ShapeDtypeStruct((ROWS + CHUNK, 1024), jnp.bfloat16)
    return pl.pallas_call(
        deal_kernel,
        out_shape=(out,) * PARTS,
        grid=(1,),
        in_specs=[SMEM]
        + [pl.BlockSpec((4, CELLS, 1024), lambda i: (1, 0, 0))] * QUADS
        + [pl.BlockSpec((1, CELLS, 1024), lambda i: (SLOTS - 1, 0, 0))] * QUADS,
        out_specs=(whole((ROWS + CHUNK, 1024)),) * PARTS,
        compiler_params=pltpu.CompilerParams(vmem_limit_bytes=52 * 2**20),
    )(where, *pieces, *pieces)


def shard_kernel(*refs):
    grads, rows, (out, numbers) = refs[:PARTS], refs[PARTS : 2 * PARTS], refs[2 * PARTS :]
    total = jnp.zeros((CHUNK, 1024), jnp.float32)
    for k in range(PARTS):
        out[k * ROWS : (k + 1) * ROWS, :] = rows[k][...]
        out[(PARTS + k) * ROWS : (PARTS + k + 1) * ROWS, :] = grads[k][:ROWS, :]
        total += grads[k][ROWS:, :].astype(jnp.float32)
    numbers[...] = total[:, :128]


def to_shard(grads, rows):
    return pl.pallas_call(
        shard_kernel,
        out_shape=(
            jax.ShapeDtypeStruct((SHARD, 1024), jnp.bfloat16),
            jax.ShapeDtypeStruct((CHUNK, 128), jnp.float32),
        ),
        in_specs=[VMEM] * (2 * PARTS),
        out_specs=(VMEM, VMEM),
    )(*grads, *rows)


def set_visible(where_ref, visible):
    rows = 4 * ROWS

    def seen(axis):
        cell = lax.broadcasted_iota(jnp.int32, (rows, rows), axis)
        return cell // ROWS * 2 + cell // CELLS % 2 * where_ref[1]

    same = (seen(0) == seen(1)).astype(jnp.float32)
    for i in range(4):
        visible[i * rows : (i + 1) * rows, :] = same


def spread_heads(field):
    head = lax.broadcasted_iota(jnp.int32, field.shape, 1) // HS
    return jnp.concatenate([jnp.where(head == i, field, jnp.zeros_like(field)) for i in range(4)], 0)


def gather_heads(field):
    rows = field.shape[0] // 4
    head = lax.broadcasted_iota(jnp.int32, (rows, field.shape[1]), 1) // HS
    out = field[:rows]
    for i in range(1, 4):
        out = jnp.where(head == i, field[i * rows : (i + 1) * rows], out)
    return out


def softmax_of(projected, visible, quad):
    queries, keyset, values = [projected[:, (c * 4 + quad) * 4 * HS : (c * 4 + quad + 1) * 4 * HS] for c in range(3)]
    queries = spread_heads(queries)
    scores = dot_f32(queries, keyset, ((1,), (1,))) * HS ** (-0.5)
    scores = jnp.where(visible[...] > 0, scores, MASKED)
    weights_exp = jnp.exp(scores - jnp.max(scores, -1, keepdims=True))
    return (queries, keyset, values, weights_exp / jnp.sum(weights_exp, -1, keepdims=True))


def forward_kernel(where_ref, p0, p1, p2, p3, gain1_ref, gain2_ref, win_ref, wout_ref,
                   rolled, projected, middle, n0, n1, n2, n3,
                   win, wout, normed, attended, visible, sems):
    loads = [
        pltpu.make_async_copy(win_ref.at[:, pl.ds(1024 * c, 1024)], win.at[c], sems.at[c]) for c in range(3)
    ] + [pltpu.make_async_copy(wout_ref, wout, sems.at[3])]
    for load in loads:
        load.start()
    set_visible(where_ref, visible)
    for g in range(4):
        for q, piece in enumerate((p0, p1, p2, p3)):
            rolled[g * ROWS + q * CELLS : g * ROWS + (q + 1) * CELLS, :] = piece[g]
        window = slice(g * ROWS, (g + 1) * ROWS)
        normed[window, :] = norm_rows(rolled[window, :], gain1_ref[...]).astype(jnp.bfloat16)
    for c in range(3):
        loads[c].wait()
        projected[:, c * 1024 : (c + 1) * 1024] = dot_f32(normed[...], win[c]).astype(jnp.bfloat16)
    for quad in range(HEADS // 4):
        _, _, values, probs = softmax_of(projected, visible, quad)
        mixed = gather_heads(dot_f32(probs.astype(jnp.bfloat16), values))
        attended[:, quad * 4 * HS : (quad + 1) * 4 * HS] = mixed.astype(jnp.bfloat16)
    loads[3].wait()
    produced = dot_f32(attended[...], wout[...]).astype(jnp.bfloat16)
    for g in range(4):
        window = slice(g * ROWS, (g + 1) * ROWS)
        total = rolled[window, :].astype(jnp.float32) + produced[window, :].astype(jnp.float32)
        middle[window, :] = total.astype(jnp.bfloat16)
        normed[window, :] = norm_rows(middle[window, :], gain2_ref[...]).astype(jnp.bfloat16)
    for k, out in enumerate((n0, n1, n2, n3)):
        group = (where_ref[0] + k) % PARTS
        out[...] = normed[pl.ds(pl.multiple_of(group * ROWS, ROWS), ROWS), :]


def attention_forward(where, pieces, gain1, gain2, weight_in, weight_out):
    rows = 4 * ROWS
    field = jax.ShapeDtypeStruct((rows, 1024), jnp.bfloat16)
    part = jax.ShapeDtypeStruct((ROWS, 1024), jnp.bfloat16)
    return pl.pallas_call(
        forward_kernel,
        out_shape=(field, jax.ShapeDtypeStruct((rows, 3072), jnp.bfloat16), field) + (part,) * PARTS,
        grid=(1,),
        in_specs=[SMEM]
        + [whole((4, CELLS, 1024))] * QUADS
        + [whole((1, 1024))] * 2
        + [ANY, ANY],
        out_specs=(whole((rows, 1024)), whole((rows, 3072)), whole((rows, 1024))) + (whole((ROWS, 1024)),) * PARTS,
        scratch_shapes=[
            pltpu.VMEM((3, 1024, 1024), jnp.bfloat16),
            pltpu.VMEM((1024, 1024), jnp.bfloat16),
            pltpu.VMEM((rows, 1024), jnp.bfloat16),
            pltpu.VMEM((rows, 1024), jnp.bfloat16),
            pltpu.VMEM((4 * rows, rows), jnp.float32),
            pltpu.SemaphoreType.DMA((4,)),
        ],
        compiler_params=pltpu.CompilerParams(vmem_limit_bytes=52 * 2**20),
        cost_estimate=pl.CostEstimate(flops=4 * 10**9, bytes_accessed=14 * 2**20, transcendentals=2**20),
    )(where, *pieces, gain1, gain2, weight_in, weight_out)


def backward_kernel(where_ref, r0, r1, r2, r3, c0, c1, c2, c3, middle, rolled, projected, gain1_ref, gain2_ref,
                    win_ref, wout_ref, o0, o1, o2, o3,
                    win, wout, arrived, grad_middle, grad_att, grad_proj, visible, sems):
    loads = [
        pltpu.make_async_copy(win_ref.at[:, pl.ds(1024 * c, 1024)], win.at[c], sems.at[c]) for c in range(3)
    ] + [pltpu.make_async_copy(wout_ref, wout, sems.at[3])]
    for load in loads[::-1]:
        load.start()
    set_visible(where_ref, visible)
    for k, part in enumerate((r0, r1, r2, r3)):
        group = (where_ref[0] + k) % PARTS
        arrived[pl.ds(pl.multiple_of(group * ROWS, ROWS), ROWS), :] = part[...]
    for g in range(4):
        window = slice(g * ROWS, (g + 1) * ROWS)
        cotangent = jnp.concatenate([c[g] for c in (c0, c1, c2, c3)], 0).astype(jnp.float32)
        back = norm_back(middle[window, :], gain2_ref[...], arrived[window, :].astype(jnp.float32))
        grad_middle[window, :] = (cotangent + back).astype(jnp.bfloat16)
    loads[3].wait()
    grad_att[...] = dot_f32(grad_middle[...], wout[...], ((1,), (1,))).astype(jnp.bfloat16)
    for quad in range(HEADS // 4):
        queries, keyset, values, probs = softmax_of(projected, visible, quad)
        grad_heads = spread_heads(grad_att[:, quad * 4 * HS : (quad + 1) * 4 * HS])
        grad_probs = dot_f32(grad_heads, values, ((1,), (1,)))
        grad_scores = probs * (grad_probs - jnp.sum(probs * grad_probs, -1, keepdims=True))
        scaled = (grad_scores * HS ** (-0.5)).astype(jnp.bfloat16)
        grads = (
            gather_heads(dot_f32(scaled, keyset)),
            dot_f32(scaled, queries, ((0,), (0,))),
            dot_f32(probs.astype(jnp.bfloat16), grad_heads, ((0,), (0,))),
        )
        for c in range(3):
            start = (c * 4 + quad) * 4 * HS
            grad_proj[:, start : start + 4 * HS] = grads[c].astype(jnp.bfloat16)
    for load in loads[:3]:
        load.wait()
    grad_norm = sum(
        dot_f32(grad_proj[:, c * 1024 : (c + 1) * 1024], win[c], ((1,), (1,))) for c in range(3)
    )
    for g in range(4):
        window = slice(g * ROWS, (g + 1) * ROWS)
        branch = norm_back(rolled[window, :], gain1_ref[...], grad_norm[window, :]).astype(jnp.bfloat16)
        total = grad_middle[window, :].astype(jnp.float32) + branch.astype(jnp.float32)
        for q, out in enumerate((o0, o1, o2, o3)):
            out[g] = total[q * CELLS : (q + 1) * CELLS, :].astype(jnp.bfloat16)


def attention_backward(where, returned, pieces, middle, rolled, projected, gain1, gain2, weight_in, weight_out):
    rows = 4 * ROWS
    piece = jax.ShapeDtypeStruct((4, CELLS, 1024), jnp.bfloat16)
    return pl.pallas_call(
        backward_kernel,
        out_shape=(piece,) * QUADS,
        grid=(1,),
        in_specs=[SMEM]
        + [whole((ROWS, 1024))] * PARTS
        + [whole((4, CELLS, 1024))] * QUADS
        + [whole((rows, 1024))] * 2
        + [whole((rows, 3072))]
        + [whole((1, 1024))] * 2
        + [ANY, ANY],
        out_specs=(whole((4, CELLS, 1024)),) * QUADS,
        scratch_shapes=[
            pltpu.VMEM((3, 1024, 1024), jnp.bfloat16),
            pltpu.VMEM((1024, 1024), jnp.bfloat16),
            pltpu.VMEM((rows, 1024), jnp.bfloat16),
            pltpu.VMEM((rows, 1024), jnp.bfloat16),
            pltpu.VMEM((rows, 1024), jnp.bfloat16),
            pltpu.VMEM((rows, 3072), jnp.bfloat16),
            pltpu.VMEM((4 * rows, rows), jnp.float32),
            pltpu.SemaphoreType.DMA((4,)),
        ],
        compiler_params=pltpu.CompilerParams(vmem_limit_bytes=52 * 2**20),
        cost_estimate=pl.CostEstimate(flops=6 * 10**9, bytes_accessed=14 * 2**20, transcendentals=2**20),
    )(where, *returned, *pieces, middle, rolled, projected, gain1, gain2, weight_in, weight_out)


def roll_out(pieces):
    half = WIN // 2
    stays, lat_part, lon_part, both = pieces
    shape = (pieces[0].shape[0], half, half, pieces[0].shape[-1])
    grid = lambda a: a.reshape(shape)
    upper = jnp.concatenate([grid(both), grid(lon_part)], 2)
    lower = jnp.concatenate([grid(lat_part), grid(stays)], 2)
    return jnp.concatenate([upper, lower], 1)


def spread(blocks):
    return [blocks[0]] + [turned(blocks[k], 2 * k) for k in range(1, PARTS)]


def body(
    tokens,
    cotangent,
    attention_in,
    attention_out,
    norm_attention,
    norm_expert,
    expert_up,
    expert_down,
    route_gain,
    assignment,
    slot_index,
):
    groups_n, lon_rows, lat_rows, features = tokens.shape
    lat_count = lax.axis_size("lat")
    lon_index = lax.axis_index("lon")
    lat_index = lax.axis_index("lat")
    place, core = lon_index // 2, lon_index % 2
    where = jnp.stack([place, (lat_index == lat_count - 1).astype(place.dtype)]).astype(jnp.int32)
    gain1, gain2 = norm_attention[None, :], norm_expert[None, :]

    half = WIN // 2
    named = assignment.reshape(groups_n, 2, half, 2, half).transpose(1, 3, 0, 2, 4)[::-1, ::-1]
    named = named.reshape(QUADS, groups_n, CELLS).astype(jnp.bfloat16)
    named = jnp.pad(named, ((0, 0), (0, CHUNK - groups_n), (0, features - CELLS)))
    def roll_in(parts):
        return (parts[0], moved(parts[1], 0, -1), moved(parts[2], -1, 0), moved(parts[3], -1, -1))

    first, later = pack(tokens, cotangent, route_gain[..., None], named)
    first = roll_in(first)
    dealt = deal(where, first)
    first, dealt = lax.optimization_barrier((first, dealt))
    grads = spread(dealt)

    rolled, projected, middle, *normed = attention_forward(
        where, first, gain1, gain2, attention_in, attention_out
    )
    shard, numbers = to_shard(grads, spread(normed))
    rows = lax.all_gather(shard, "lat", axis=0, tiled=True)

    numbers, expert_down, expert_up, later = lax.optimization_barrier((numbers, expert_down, expert_up, later))
    ups, downs = (expert_up, swapped(expert_up, "lon", 1)), (expert_down, swapped(expert_down, "lon", 1))
    later = roll_in(later)

    numbers, later = lax.optimization_barrier((numbers, later))
    numbers = lax.all_gather(numbers.astype(jnp.int32), "lat", axis=0)
    numbers = numbers[:, :, :CELLS].reshape(lat_count, PARTS * ROWS) ^ (4 * core)
    places, plans, slots, slots_t, counts = zip(*[routes(numbers[TILES * h : TILES * (h + 1)]) for h in range(2)])

    back, *arrays = expert_side(
        jnp.concatenate(places, 0), jnp.stack(plans), rows, ups, downs,
        jnp.concatenate(slots, 0), jnp.concatenate(slots_t, 1),
    )
    summed = lax.psum_scatter(back, "lat", scatter_dimension=0, tiled=True)
    came = [swapped(a, "lon", 1) for a in weight_side(weight_plan(counts, 1), arrays)]
    grad_up, grad_down = weight_side(weight_plan(counts, 0), arrays, came)

    summed, grad_up, grad_down = lax.optimization_barrier((summed, grad_up, grad_down))
    summed = [summed[k * ROWS : (k + 1) * ROWS] for k in range(PARTS)]
    returned = [summed[0]] + [turned(summed[k], -2 * k) for k in range(1, PARTS)]
    out = attention_backward(
        where, returned, later, middle, rolled, projected, gain1, gain2, attention_in, attention_out
    )
    came = [moved(out[1], 0, 1), moved(out[2], 1, 0), moved(out[3], 1, 1)]
    return (roll_out([out[0], *came]), grad_up, grad_down)


def solution(mesh):
    return jax.shard_map(
        body,
        mesh=mesh,
        in_specs=(
            P(None, "lon", "lat", None),
            P(None, "lon", "lat", None),
            P(),
            P(),
            P(),
            P(),
            P("lon", None, "lat"),
            P("lon", "lat", None),
            P(None, "lon", "lat"),
            P(None, "lon", "lat"),
            P(None, "lon", "lat"),
        ),
        out_specs=(P(None, "lon", "lat", None), P("lon", None, "lat"), P("lon", "lat", None)),
        check_vma=False,
    )
```

```python
import functools
import math

import jax
import jax.numpy as jnp
from jax import lax
from jax.experimental import pallas as pl
from jax.experimental.pallas import tpu as pltpu
from jax.sharding import PartitionSpec as P

HS = 64
EPG = 8
WIN = 8
EPSILON = 1e-06
TANH_SCALE = math.sqrt(2.0 / math.pi)
CUBIC_COEF = 0.044715
MASKED = -1000000000.0

PARTS = 4
ROWS = 64
TILE = 256
CHUNK = 16
TILE_CHUNKS = 24
TILES = 8
BLOCK = 256
BLOCKS = 21
SPARE = (BLOCKS - 1) * (BLOCK // CHUNK)
STEPS = 2 * 19
AHEAD = 4
BACKS = 4
RING = 4
HEADS = 16
QUADS = 4
CELLS = 16
SLOTS = 9
SHARD = 2 * PARTS * ROWS
BUFFER = BLOCKS * BLOCK

ANY = pl.BlockSpec(memory_space=pl.ANY)
SMEM = pl.BlockSpec(memory_space=pltpu.SMEM)
VMEM = pl.BlockSpec(memory_space=pltpu.VMEM)


def swapped(block, axis, direction):
    return lax.ppermute(block, axis, [(i, i ^ direction) for i in range(lax.axis_size(axis))])


def turned(block, distance):
    devices = lax.axis_size("lon")
    return lax.ppermute(block, "lon", [(i, (i + distance) % devices) for i in range(devices)])


def moved(block, lon_step, lat_step):
    lons, lats = lax.axis_size("lon"), lax.axis_size("lat")
    route = [
        (i * lats + j, (i + lon_step) % lons * lats + (j + lat_step) % lats)
        for i in range(lons)
        for j in range(lats)
    ]
    return lax.ppermute(block, ("lon", "lat"), route)


def gelu_parts(preact):
    argument = TANH_SCALE * (preact + CUBIC_COEF * preact * preact * preact)
    tangent = jnp.tanh(argument)
    activated = 0.5 * preact * (1.0 + tangent)
    derivative = 0.5 * (1.0 + tangent) + 0.5 * preact * (1.0 - tangent * tangent) * TANH_SCALE * (
        1.0 + 3.0 * CUBIC_COEF * preact * preact
    )
    return (activated, derivative)


def norm_rows(field, gain_vec):
    values_f = field.astype(jnp.float32)
    factor = lax.rsqrt(jnp.mean(values_f * values_f, -1, keepdims=True) + EPSILON)
    return values_f * factor * gain_vec


def norm_back(field, gain_vec, grad_in):
    values_f = field.astype(jnp.float32)
    factor = lax.rsqrt(jnp.mean(values_f * values_f, -1, keepdims=True) + EPSILON)
    scaled_grad = grad_in * gain_vec
    inner_mean = jnp.mean(values_f * scaled_grad, -1, keepdims=True)
    return factor * scaled_grad - values_f * factor * factor * factor * inner_mean


def dot_f32(a, b, contract=((1,), (0,))):
    return lax.dot_general(a, b, (contract, ((), ())), preferred_element_type=jnp.float32)


def block_rows(index):
    return pl.ds(pl.multiple_of(index * BLOCK, BLOCK), BLOCK)


def chunk_rows(index):
    return pl.ds(pl.multiple_of(index * CHUNK, CHUNK), CHUNK)


def expert_kernel(place_ref, plan_ref, all_ref, up_own_ref, up_other_ref, down_own_ref, down_other_ref,
                  slots_row_ref, slots_col_ref,
                  back_ref, rows_out_ref, grads_out_ref, hidden_ref, gpre_ref,
                  raw, raw_grad, up, down, rows, grads, result, hidden, gpre, stage, back,
                  raw_sem, raw_grad_sem, weight_sem, rows_sem, grads_sem, hidden_sem, gpre_sem, back_sem):
    def tile(t):
        return pl.ds(t * TILE, TILE)

    def row_loads(n):
        slot = n % RING
        return [
            pltpu.make_async_copy(all_ref.at[pl.ds(n * SHARD + first, TILE)], target.at[slot], sem.at[slot])
            for first, target, sem in ((0, raw, raw_sem), (TILE, raw_grad, raw_grad_sem))
        ]

    def begin(n):
        if n < 2 * TILES:
            for load in row_loads(n):
                load.start()

    weight_loads = [
        pltpu.make_async_copy(up_own_ref, up.at[pl.ds(0, 4)], weight_sem.at[0]),
        pltpu.make_async_copy(up_other_ref, up.at[pl.ds(4, 4)], weight_sem.at[1]),
        pltpu.make_async_copy(down_own_ref, down.at[pl.ds(0, 4)], weight_sem.at[2]),
        pltpu.make_async_copy(down_other_ref, down.at[pl.ds(4, 4)], weight_sem.at[3]),
    ]
    for n in range(RING):
        begin(n)
    for load in weight_loads:
        load.start()

    def clear(b, carry):
        for buffer in (rows, grads):
            buffer[block_rows(b), :] = jnp.zeros((BLOCK, buffer.shape[1]), buffer.dtype)
        return carry

    result[SPARE * CHUNK : (SPARE + 1) * CHUNK, :] = jnp.zeros((CHUNK, result.shape[1]), result.dtype)
    backs = []
    for h in range(2):
        count = (plan_ref[h, BLOCKS] + 1) // 2 * 2

        def wide_stores(b):
            target = block_rows(h * BLOCKS + b)
            return [
                pltpu.make_async_copy(rows.at[block_rows(b)], rows_out_ref.at[target], rows_sem.at[b]),
                pltpu.make_async_copy(grads.at[block_rows(b)], grads_out_ref.at[target], grads_sem.at[b]),
            ]

        def narrow_stores(b):
            target = block_rows(h * BLOCKS + b)
            return [
                pltpu.make_async_copy(hidden.at[b % RING], hidden_ref.at[target], hidden_sem.at[b % RING]),
                pltpu.make_async_copy(gpre.at[b % RING], gpre_ref.at[target], gpre_sem.at[b % RING]),
            ]

        lax.fori_loop(0, count, clear, 0)
        spots = lax.broadcasted_iota(jnp.int32, (TILE_CHUNKS * CHUNK, TILE), 0)
        for n in range(h * TILES, (h + 1) * TILES):
            pick = (spots == slots_row_ref[n : n + 1, :]).astype(jnp.bfloat16)
            for load, source, buffer in zip(row_loads(n), (raw, raw_grad), (rows, grads)):
                load.wait()
                packed = dot_f32(pick, source[n % RING]).astype(jnp.bfloat16)
                for q in range(TILE_CHUNKS):
                    buffer[chunk_rows(place_ref[n, q]), :] = packed[q * CHUNK : (q + 1) * CHUNK]
            begin(n + RING)
        if h == 0:
            for load in weight_loads:
                load.wait()

        def step(pair, carry):
            both = (2 * pair, 2 * pair + 1)

            @pl.when(pair >= 2)
            def _():
                for b in both:
                    for store in narrow_stores(b - RING):
                        store.wait()

            preacts = [dot_f32(rows[block_rows(b), :], up[plan_ref[h, b]]) for b in both]
            grad_hiddens = [dot_f32(grads[block_rows(b), :], down[plan_ref[h, b]], ((1,), (1,))) for b in both]
            for b, preact, grad_hidden in zip(both, preacts, grad_hiddens):
                activated, derivative = gelu_parts(preact)
                hidden[b % RING] = activated.astype(jnp.bfloat16)
                grad_pre = (grad_hidden * derivative).astype(jnp.bfloat16)
                gpre[b % RING] = grad_pre
                result[block_rows(b), :] = dot_f32(grad_pre, up[plan_ref[h, b]], ((1,), (1,))).astype(jnp.bfloat16)
                for store in wide_stores(b) + narrow_stores(b):
                    store.start()
            return carry

        lax.fori_loop(0, count // 2, step, 0)

        spots = lax.broadcasted_iota(jnp.int32, (TILE, TILE_CHUNKS * CHUNK), 1)
        for t in range(TILES):
            n = h * TILES + t
            for q in range(TILE_CHUNKS):
                stage[q * CHUNK : (q + 1) * CHUNK, :] = result[chunk_rows(place_ref[n, q]), :]
            pick = (spots == slots_col_ref[:, n : n + 1]).astype(jnp.bfloat16)
            if n >= BACKS:
                backs[n - BACKS].wait()
            back[n % BACKS] = dot_f32(pick, stage[...]).astype(jnp.bfloat16)
            backs.append(pltpu.make_async_copy(back.at[n % BACKS], back_ref.at[tile(n)], back_sem.at[n % BACKS]))
            backs[n].start()

        def finish(b, carry):
            for store in wide_stores(b):
                store.wait()

            @pl.when(b >= count - RING)
            def _():
                for store in narrow_stores(b):
                    store.wait()

            return carry

        lax.fori_loop(0, count, finish, 0)
    for store in backs[-BACKS:]:
        store.wait()


def expert_side(place, plan, rows, ups, downs, slots_row, slots_col):
    features, hidden_units = ups[0].shape[1:]
    wide = jax.ShapeDtypeStruct((2 * BUFFER, features), jnp.bfloat16)
    narrow = jax.ShapeDtypeStruct((2 * BUFFER, hidden_units), jnp.bfloat16)
    blocks_sem, ring_sem = pltpu.SemaphoreType.DMA((BLOCKS,)), pltpu.SemaphoreType.DMA((RING,))
    return pl.pallas_call(
        expert_kernel,
        out_shape=(jax.ShapeDtypeStruct((2 * TILES * TILE, features), jnp.bfloat16), wide, wide, narrow, narrow),
        in_specs=[SMEM] * 2 + [ANY] * 5 + [VMEM, VMEM],
        out_specs=(ANY,) * 5,
        scratch_shapes=[
            pltpu.VMEM((RING, TILE, features), jnp.bfloat16),
            pltpu.VMEM((RING, TILE, features), jnp.bfloat16),
            pltpu.VMEM((EPG, features, hidden_units), jnp.bfloat16),
            pltpu.VMEM((EPG, hidden_units, features), jnp.bfloat16),
            pltpu.VMEM((BUFFER, features), jnp.bfloat16),
            pltpu.VMEM((BUFFER, features), jnp.bfloat16),
            pltpu.VMEM((BUFFER, features), jnp.bfloat16),
            pltpu.VMEM((RING, BLOCK, hidden_units), jnp.bfloat16),
            pltpu.VMEM((RING, BLOCK, hidden_units), jnp.bfloat16),
            pltpu.VMEM((TILE_CHUNKS * CHUNK, features), jnp.bfloat16),
            pltpu.VMEM((BACKS, TILE, features), jnp.bfloat16),
            ring_sem,
            ring_sem,
            ring_sem,
            blocks_sem,
            blocks_sem,
            ring_sem,
            ring_sem,
            pltpu.SemaphoreType.DMA((BACKS,)),
        ],
        compiler_params=pltpu.CompilerParams(vmem_limit_bytes=52 * 2**20),
        cost_estimate=pl.CostEstimate(flops=30 * 10**9, bytes_accessed=64 * 2**20, transcendentals=2 * 10**6),
    )(place, plan, rows, *ups, *downs, slots_row, slots_col)


def weight_kernel(start_ref, block_ref, *refs):
    arrays, before = refs[:4], refs[4:-8]
    (up_ref, down_ref), buffers, (total, sems) = refs[-8:-6], refs[-6:-2], refs[-2:]
    expert = pl.program_id(0)
    count = start_ref[4]

    def loads(i):
        return [
            pltpu.make_async_copy(a.at[block_rows(block_ref[i])], buffer.at[i % AHEAD], sems.at[n, i % AHEAD])
            for n, (a, buffer) in enumerate(zip(arrays, buffers))
        ]

    def begin(i):
        @pl.when(i < count)
        def _():
            for load in loads(i):
                load.start()

    @pl.when(expert == 0)
    def _():
        for i in range(AHEAD - 1):
            begin(jnp.int32(i))

    total[...] = jnp.zeros_like(total)
    down_ref[...] = before[1][...] if before else jnp.zeros_like(down_ref)

    def step(i, carry):
        for load in loads(i):
            load.wait()
        begin(i + AHEAD - 1)
        rows, grads, hidden, gpre = [buffer[i % AHEAD] for buffer in buffers]
        total[...] += dot_f32(gpre, rows, ((0,), (0,)))
        down_ref[0] += dot_f32(hidden, grads, ((0,), (0,)))
        return carry

    lax.fori_loop(start_ref[expert], start_ref[expert + 1], step, 0)
    up_ref[0] = total[...].T + (before[0][0] if before else 0.0)


def weight_side(plan, arrays, before=()):
    features, hidden_units = arrays[0].shape[1], arrays[2].shape[1]
    up, down = (features, hidden_units), (hidden_units, features)
    outs = tuple(pl.BlockSpec((1, *shape), lambda e: (e, 0, 0)) for shape in (up, down))
    return pl.pallas_call(
        weight_kernel,
        out_shape=tuple(jax.ShapeDtypeStruct((4, *shape), jnp.float32) for shape in (up, down)),
        grid=(4,),
        in_specs=[SMEM] * 2 + [ANY] * 4 + list(outs[: len(before)]),
        out_specs=outs,
        scratch_shapes=[pltpu.VMEM((AHEAD, BLOCK, a.shape[1]), jnp.bfloat16) for a in arrays]
        + [pltpu.VMEM(down, jnp.float32), pltpu.SemaphoreType.DMA((4, AHEAD))],
        compiler_params=pltpu.CompilerParams(vmem_limit_bytes=52 * 2**20),
        cost_estimate=pl.CostEstimate(flops=4 * 10**9, bytes_accessed=25 * 2**20, transcendentals=0),
    )(*plan, *arrays, *before)


def weight_plan(counts, side):
    ahead = lambda v: jnp.cumsum(v) - v
    mine = slice(4 * side, 4 * side + 4)
    halves = [(ahead(c)[mine][None, :] + h * BLOCKS, c[mine][None, :]) for h, c in enumerate(counts)]
    totals = (halves[0][1] + halves[1][1])[0]
    starts = ahead(totals)
    step = jnp.arange(STEPS, dtype=jnp.int32)[:, None]
    inside = (step >= starts[None, :]) & (step < (starts + totals)[None, :])
    offset = step - starts[None, :]
    block = jnp.where(offset >= halves[0][1], halves[1][0] + offset - halves[0][1], halves[0][0] + offset)
    block = jnp.sum(jnp.where(inside, block, 0), 1)
    return (jnp.concatenate([starts, jnp.sum(totals)[None]]).astype(jnp.int32), block.astype(jnp.int32))


def routes(named):
    onehot = (named[..., None] == jnp.arange(EPG)).astype(jnp.bfloat16)
    earlier = jnp.tril(jnp.ones((TILE, TILE), jnp.bfloat16), -1)
    ranks = jnp.einsum("rs,tse->tre", earlier, onehot, preferred_element_type=jnp.float32)
    onehot_f = onehot.astype(jnp.float32)
    rank = jnp.sum(ranks * onehot_f, -1).astype(jnp.int32)
    counts = jnp.sum(onehot_f, 1).astype(jnp.int32)
    chunks = (counts + CHUNK - 1) // CHUNK

    def before(values, axis):
        return jnp.cumsum(values, axis) - values

    starts = before(chunks, 1)
    slots = CHUNK * jnp.sum(onehot_f * starts[:, None, :].astype(jnp.float32), -1).astype(jnp.int32) + rank
    per_block = BLOCK // CHUNK
    blocks = jnp.maximum((jnp.sum(chunks, 0) + per_block - 1) // per_block, 1)
    first_block = before(blocks, 0)
    places = first_block[None, :] * per_block + before(chunks, 0)
    index = jnp.arange(TILE_CHUNKS)[None, :, None]
    inside = (index >= starts[:, None, :]) & (index < (starts + chunks)[:, None, :])
    place = jnp.sum(jnp.where(inside, places[:, None, :] + index - starts[:, None, :] - SPARE, 0), -1) + SPARE
    number = jnp.arange(BLOCKS)[:, None]
    plan = jnp.sum((number >= first_block[None, :]).astype(jnp.int32), -1) - 1
    plan = jnp.concatenate([plan, jnp.sum(blocks)[None]]).astype(jnp.int32)
    return (place.astype(jnp.int32), plan, slots, slots.T, blocks)


def whole(shape):
    return pl.BlockSpec(shape, lambda i: (0,) * len(shape))


def pack_kernel(tokens_ref, cotangent_ref, gain_ref, named_ref, *refs):
    outs, later, scratch = refs[:QUADS], refs[QUADS : 2 * QUADS], refs[2 * QUADS]
    half = WIN // 2
    corners = ((half, half), (half, 0), (0, half), (0, 0))
    for g in range(tokens_ref.shape[0]):
        cotangent_f = cotangent_ref[g].astype(jnp.float32)
        fields = (tokens_ref[g].astype(jnp.float32), gain_ref[g] * cotangent_f, cotangent_f)
        for f, field in enumerate(fields):
            for q, (lon, lat) in enumerate(corners):
                for i in range(half):
                    scratch[f, q, half * i : half * (i + 1), :] = field[lon + i, lat : lat + half, :]
        for q in range(QUADS):
            outs[q][g] = scratch[0, q].astype(jnp.bfloat16)
            outs[q][4 + g] = scratch[1, q].astype(jnp.bfloat16)
            later[q][g] = scratch[2, q].astype(jnp.bfloat16)
    for q in range(QUADS):
        outs[q][SLOTS - 1] = named_ref[q]


def pack(tokens, cotangent, gain, named):
    features = tokens.shape[-1]
    piece = jax.ShapeDtypeStruct((SLOTS, CELLS, features), jnp.bfloat16)
    later = jax.ShapeDtypeStruct((4, CELLS, features), jnp.bfloat16)
    outs = pl.pallas_call(
        pack_kernel,
        out_shape=(piece,) * QUADS + (later,) * QUADS,
        in_specs=[VMEM] * 4,
        out_specs=(VMEM,) * (2 * QUADS),
        scratch_shapes=[pltpu.VMEM((3, QUADS, CELLS, features), jnp.float32)],
        compiler_params=pltpu.CompilerParams(vmem_limit_bytes=52 * 2**20),
    )(tokens, cotangent, gain, named)
    return (outs[:QUADS], outs[QUADS:])


def deal_kernel(where_ref, *refs):
    grads, named, outs = refs[:QUADS], refs[QUADS : 2 * QUADS], refs[2 * QUADS :]
    row = lax.broadcasted_iota(jnp.int32, (CHUNK, 1024), 0)
    for k in range(PARTS):
        group = (where_ref[0] + k) % PARTS
        numbers = jnp.zeros((CHUNK, 1024), jnp.float32)
        for q in range(QUADS):
            outs[k][q * CELLS : (q + 1) * CELLS, :] = grads[q][group]
            line = jnp.sum(jnp.where(row == group, named[q][0].astype(jnp.float32), 0.0), 0, keepdims=True)
            numbers += jnp.where(row == QUADS * k + q, line, 0.0)
        outs[k][ROWS : ROWS + CHUNK, :] = numbers.astype(jnp.bfloat16)


def deal(where, pieces):
    out = jax.ShapeDtypeStruct((ROWS + CHUNK, 1024), jnp.bfloat16)
    return pl.pallas_call(
        deal_kernel,
        out_shape=(out,) * PARTS,
        grid=(1,),
        in_specs=[SMEM]
        + [pl.BlockSpec((4, CELLS, 1024), lambda i: (1, 0, 0))] * QUADS
        + [pl.BlockSpec((1, CELLS, 1024), lambda i: (SLOTS - 1, 0, 0))] * QUADS,
        out_specs=(whole((ROWS + CHUNK, 1024)),) * PARTS,
        compiler_params=pltpu.CompilerParams(vmem_limit_bytes=52 * 2**20),
    )(where, *pieces, *pieces)


def shard_kernel(*refs):
    grads, rows, (out, numbers) = refs[:PARTS], refs[PARTS : 2 * PARTS], refs[2 * PARTS :]
    total = jnp.zeros((CHUNK, 1024), jnp.float32)
    for k in range(PARTS):
        out[k * ROWS : (k + 1) * ROWS, :] = rows[k][...]
        out[(PARTS + k) * ROWS : (PARTS + k + 1) * ROWS, :] = grads[k][:ROWS, :]
        total += grads[k][ROWS:, :].astype(jnp.float32)
    numbers[...] = total[:, :128]


def to_shard(grads, rows):
    return pl.pallas_call(
        shard_kernel,
        out_shape=(
            jax.ShapeDtypeStruct((SHARD, 1024), jnp.bfloat16),
            jax.ShapeDtypeStruct((CHUNK, 128), jnp.float32),
        ),
        in_specs=[VMEM] * (2 * PARTS),
        out_specs=(VMEM, VMEM),
    )(*grads, *rows)


def set_visible(where_ref, visible):
    rows = 4 * ROWS

    def seen(axis):
        cell = lax.broadcasted_iota(jnp.int32, (rows, rows), axis)
        return cell // ROWS * 2 + cell // CELLS % 2 * where_ref[1]

    same = (seen(0) == seen(1)).astype(jnp.float32)
    for i in range(4):
        visible[i * rows : (i + 1) * rows, :] = same


def spread_heads(field):
    head = lax.broadcasted_iota(jnp.int32, field.shape, 1) // HS
    return jnp.concatenate([jnp.where(head == i, field, jnp.zeros_like(field)) for i in range(4)], 0)


def gather_heads(field):
    rows = field.shape[0] // 4
    head = lax.broadcasted_iota(jnp.int32, (rows, field.shape[1]), 1) // HS
    out = field[:rows]
    for i in range(1, 4):
        out = jnp.where(head == i, field[i * rows : (i + 1) * rows], out)
    return out


def softmax_of(projected, visible, quad):
    queries, keyset, values = [projected[:, (c * 4 + quad) * 4 * HS : (c * 4 + quad + 1) * 4 * HS] for c in range(3)]
    queries = spread_heads(queries)
    scores = dot_f32(queries, keyset, ((1,), (1,))) * HS ** (-0.5)
    scores = jnp.where(visible[...] > 0, scores, MASKED)
    weights_exp = jnp.exp(scores - jnp.max(scores, -1, keepdims=True))
    return (queries, keyset, values, weights_exp / jnp.sum(weights_exp, -1, keepdims=True))


def forward_kernel(where_ref, p0, p1, p2, p3, gain1_ref, gain2_ref, win_ref, wout_ref,
                   rolled, projected, middle, n0, n1, n2, n3,
                   win, wout, normed, attended, visible, sems):
    loads = [
        pltpu.make_async_copy(win_ref.at[:, pl.ds(1024 * c, 1024)], win.at[c], sems.at[c]) for c in range(3)
    ] + [pltpu.make_async_copy(wout_ref, wout, sems.at[3])]
    for load in loads:
        load.start()
    set_visible(where_ref, visible)
    for g in range(4):
        for q, piece in enumerate((p0, p1, p2, p3)):
            rolled[g * ROWS + q * CELLS : g * ROWS + (q + 1) * CELLS, :] = piece[g]
        window = slice(g * ROWS, (g + 1) * ROWS)
        normed[window, :] = norm_rows(rolled[window, :], gain1_ref[...]).astype(jnp.bfloat16)
    for c in range(3):
        loads[c].wait()
        projected[:, c * 1024 : (c + 1) * 1024] = dot_f32(normed[...], win[c]).astype(jnp.bfloat16)
    for quad in range(HEADS // 4):
        _, _, values, probs = softmax_of(projected, visible, quad)
        mixed = gather_heads(dot_f32(probs.astype(jnp.bfloat16), values))
        attended[:, quad * 4 * HS : (quad + 1) * 4 * HS] = mixed.astype(jnp.bfloat16)
    loads[3].wait()
    produced = dot_f32(attended[...], wout[...]).astype(jnp.bfloat16)
    for g in range(4):
        window = slice(g * ROWS, (g + 1) * ROWS)
        total = rolled[window, :].astype(jnp.float32) + produced[window, :].astype(jnp.float32)
        middle[window, :] = total.astype(jnp.bfloat16)
        normed[window, :] = norm_rows(middle[window, :], gain2_ref[...]).astype(jnp.bfloat16)
    for k, out in enumerate((n0, n1, n2, n3)):
        group = (where_ref[0] + k) % PARTS
        out[...] = normed[pl.ds(pl.multiple_of(group * ROWS, ROWS), ROWS), :]


def attention_forward(where, pieces, gain1, gain2, weight_in, weight_out):
    rows = 4 * ROWS
    field = jax.ShapeDtypeStruct((rows, 1024), jnp.bfloat16)
    part = jax.ShapeDtypeStruct((ROWS, 1024), jnp.bfloat16)
    return pl.pallas_call(
        forward_kernel,
        out_shape=(field, jax.ShapeDtypeStruct((rows, 3072), jnp.bfloat16), field) + (part,) * PARTS,
        grid=(1,),
        in_specs=[SMEM]
        + [whole((4, CELLS, 1024))] * QUADS
        + [whole((1, 1024))] * 2
        + [ANY, ANY],
        out_specs=(whole((rows, 1024)), whole((rows, 3072)), whole((rows, 1024))) + (whole((ROWS, 1024)),) * PARTS,
        scratch_shapes=[
            pltpu.VMEM((3, 1024, 1024), jnp.bfloat16),
            pltpu.VMEM((1024, 1024), jnp.bfloat16),
            pltpu.VMEM((rows, 1024), jnp.bfloat16),
            pltpu.VMEM((rows, 1024), jnp.bfloat16),
            pltpu.VMEM((4 * rows, rows), jnp.float32),
            pltpu.SemaphoreType.DMA((4,)),
        ],
        compiler_params=pltpu.CompilerParams(vmem_limit_bytes=52 * 2**20),
        cost_estimate=pl.CostEstimate(flops=4 * 10**9, bytes_accessed=14 * 2**20, transcendentals=2**20),
    )(where, *pieces, gain1, gain2, weight_in, weight_out)


def backward_kernel(where_ref, r0, r1, r2, r3, c0, c1, c2, c3, middle, rolled, projected, gain1_ref, gain2_ref,
                    win_ref, wout_ref, o0, o1, o2, o3,
                    win, wout, arrived, grad_middle, grad_att, grad_proj, visible, sems):
    loads = [
        pltpu.make_async_copy(win_ref.at[:, pl.ds(1024 * c, 1024)], win.at[c], sems.at[c]) for c in range(3)
    ] + [pltpu.make_async_copy(wout_ref, wout, sems.at[3])]
    for load in loads[::-1]:
        load.start()
    set_visible(where_ref, visible)
    for k, part in enumerate((r0, r1, r2, r3)):
        group = (where_ref[0] + k) % PARTS
        arrived[pl.ds(pl.multiple_of(group * ROWS, ROWS), ROWS), :] = part[...]
    for g in range(4):
        window = slice(g * ROWS, (g + 1) * ROWS)
        cotangent = jnp.concatenate([c[g] for c in (c0, c1, c2, c3)], 0).astype(jnp.float32)
        back = norm_back(middle[window, :], gain2_ref[...], arrived[window, :].astype(jnp.float32))
        grad_middle[window, :] = (cotangent + back).astype(jnp.bfloat16)
    loads[3].wait()
    grad_att[...] = dot_f32(grad_middle[...], wout[...], ((1,), (1,))).astype(jnp.bfloat16)
    for quad in range(HEADS // 4):
        queries, keyset, values, probs = softmax_of(projected, visible, quad)
        grad_heads = spread_heads(grad_att[:, quad * 4 * HS : (quad + 1) * 4 * HS])
        grad_probs = dot_f32(grad_heads, values, ((1,), (1,)))
        grad_scores = probs * (grad_probs - jnp.sum(probs * grad_probs, -1, keepdims=True))
        scaled = (grad_scores * HS ** (-0.5)).astype(jnp.bfloat16)
        grads = (
            gather_heads(dot_f32(scaled, keyset)),
            dot_f32(scaled, queries, ((0,), (0,))),
            dot_f32(probs.astype(jnp.bfloat16), grad_heads, ((0,), (0,))),
        )
        for c in range(3):
            start = (c * 4 + quad) * 4 * HS
            grad_proj[:, start : start + 4 * HS] = grads[c].astype(jnp.bfloat16)
    for load in loads[:3]:
        load.wait()
    grad_norm = sum(
        dot_f32(grad_proj[:, c * 1024 : (c + 1) * 1024], win[c], ((1,), (1,))) for c in range(3)
    )
    for g in range(4):
        window = slice(g * ROWS, (g + 1) * ROWS)
        branch = norm_back(rolled[window, :], gain1_ref[...], grad_norm[window, :]).astype(jnp.bfloat16)
        total = grad_middle[window, :].astype(jnp.float32) + branch.astype(jnp.float32)
        for q, out in enumerate((o0, o1, o2, o3)):
            out[g] = total[q * CELLS : (q + 1) * CELLS, :].astype(jnp.bfloat16)


def attention_backward(where, returned, pieces, middle, rolled, projected, gain1, gain2, weight_in, weight_out):
    rows = 4 * ROWS
    piece = jax.ShapeDtypeStruct((4, CELLS, 1024), jnp.bfloat16)
    return pl.pallas_call(
        backward_kernel,
        out_shape=(piece,) * QUADS,
        grid=(1,),
        in_specs=[SMEM]
        + [whole((ROWS, 1024))] * PARTS
        + [whole((4, CELLS, 1024))] * QUADS
        + [whole((rows, 1024))] * 2
        + [whole((rows, 3072))]
        + [whole((1, 1024))] * 2
        + [ANY, ANY],
        out_specs=(whole((4, CELLS, 1024)),) * QUADS,
        scratch_shapes=[
            pltpu.VMEM((3, 1024, 1024), jnp.bfloat16),
            pltpu.VMEM((1024, 1024), jnp.bfloat16),
            pltpu.VMEM((rows, 1024), jnp.bfloat16),
            pltpu.VMEM((rows, 1024), jnp.bfloat16),
            pltpu.VMEM((rows, 1024), jnp.bfloat16),
            pltpu.VMEM((rows, 3072), jnp.bfloat16),
            pltpu.VMEM((4 * rows, rows), jnp.float32),
            pltpu.SemaphoreType.DMA((4,)),
        ],
        compiler_params=pltpu.CompilerParams(vmem_limit_bytes=52 * 2**20),
        cost_estimate=pl.CostEstimate(flops=6 * 10**9, bytes_accessed=14 * 2**20, transcendentals=2**20),
    )(where, *returned, *pieces, middle, rolled, projected, gain1, gain2, weight_in, weight_out)


def roll_out(pieces):
    half = WIN // 2
    stays, lat_part, lon_part, both = pieces
    shape = (pieces[0].shape[0], half, half, pieces[0].shape[-1])
    grid = lambda a: a.reshape(shape)
    upper = jnp.concatenate([grid(both), grid(lon_part)], 2)
    lower = jnp.concatenate([grid(lat_part), grid(stays)], 2)
    return jnp.concatenate([upper, lower], 1)


def spread(blocks):
    return [blocks[0]] + [turned(blocks[k], 2 * k) for k in range(1, PARTS)]


def body(
    tokens,
    cotangent,
    attention_in,
    attention_out,
    norm_attention,
    norm_expert,
    expert_up,
    expert_down,
    route_gain,
    assignment,
    slot_index,
):
    groups_n, lon_rows, lat_rows, features = tokens.shape
    lat_count = lax.axis_size("lat")
    lon_index = lax.axis_index("lon")
    lat_index = lax.axis_index("lat")
    place, core = lon_index // 2, lon_index % 2
    where = jnp.stack([place, (lat_index == lat_count - 1).astype(place.dtype)]).astype(jnp.int32)
    gain1, gain2 = norm_attention[None, :], norm_expert[None, :]

    half = WIN // 2
    named = assignment.reshape(groups_n, 2, half, 2, half).transpose(1, 3, 0, 2, 4)[::-1, ::-1]
    named = named.reshape(QUADS, groups_n, CELLS).astype(jnp.bfloat16)
    named = jnp.pad(named, ((0, 0), (0, CHUNK - groups_n), (0, features - CELLS)))
    def roll_in(parts):
        return (parts[0], moved(parts[1], 0, -1), moved(parts[2], -1, 0), moved(parts[3], -1, -1))

    first, later = pack(tokens, cotangent, route_gain[..., None], named)
    first = roll_in(first)
    dealt = deal(where, first)
    first, dealt = lax.optimization_barrier((first, dealt))
    grads = spread(dealt)

    rolled, projected, middle, *normed = attention_forward(
        where, first, gain1, gain2, attention_in, attention_out
    )
    normed, grads = lax.optimization_barrier((normed, grads))
    shard, numbers = to_shard(grads, spread(normed))
    rows = lax.all_gather(shard, "lat", axis=0, tiled=True)

    numbers, expert_down, expert_up, later = lax.optimization_barrier((numbers, expert_down, expert_up, later))
    ups, downs = (expert_up, swapped(expert_up, "lon", 1)), (expert_down, swapped(expert_down, "lon", 1))
    later = roll_in(later)

    numbers, later = lax.optimization_barrier((numbers, later))
    numbers = lax.all_gather(numbers.astype(jnp.int32), "lat", axis=0)
    numbers = numbers[:, :, :CELLS].reshape(lat_count, PARTS * ROWS) ^ (4 * core)
    places, plans, slots, slots_t, counts = zip(*[routes(numbers[TILES * h : TILES * (h + 1)]) for h in range(2)])

    back, *arrays = expert_side(
        jnp.concatenate(places, 0), jnp.stack(plans), rows, ups, downs,
        jnp.concatenate(slots, 0), jnp.concatenate(slots_t, 1),
    )
    summed = lax.psum_scatter(back, "lat", scatter_dimension=0, tiled=True)
    came = [swapped(a, "lon", 1) for a in weight_side(weight_plan(counts, 1), arrays)]
    grad_up, grad_down = weight_side(weight_plan(counts, 0), arrays, came)

    summed, grad_up, grad_down = lax.optimization_barrier((summed, grad_up, grad_down))
    summed = [summed[k * ROWS : (k + 1) * ROWS] for k in range(PARTS)]
    returned = [summed[0]] + [turned(summed[k], -2 * k) for k in range(1, PARTS)]
    out = attention_backward(
        where, returned, later, middle, rolled, projected, gain1, gain2, attention_in, attention_out
    )
    came = [moved(out[1], 0, 1), moved(out[2], 1, 0), moved(out[3], 1, 1)]
    return (roll_out([out[0], *came]), grad_up, grad_down)


def solution(mesh):
    return jax.shard_map(
        body,
        mesh=mesh,
        in_specs=(
            P(None, "lon", "lat", None),
            P(None, "lon", "lat", None),
            P(),
            P(),
            P(),
            P(),
            P("lon", None, "lat"),
            P("lon", "lat", None),
            P(None, "lon", "lat"),
            P(None, "lon", "lat"),
            P(None, "lon", "lat"),
        ),
        out_specs=(P(None, "lon", "lat", None), P("lon", None, "lat"), P("lon", "lat", None)),
        check_vma=False,
    )
```

```python
import functools
import math

import jax
import jax.numpy as jnp
from jax import lax
from jax.experimental import pallas as pl
from jax.experimental.pallas import tpu as pltpu
from jax.sharding import PartitionSpec as P

HS = 64
EPG = 8
WIN = 8
EPSILON = 1e-06
TANH_SCALE = math.sqrt(2.0 / math.pi)
CUBIC_COEF = 0.044715
MASKED = -1000000000.0

PARTS = 4
ROWS = 64
TILE = 256
CHUNK = 16
TILE_CHUNKS = 24
TILES = 8
BLOCK = 256
BLOCKS = 21
SPARE = (BLOCKS - 1) * (BLOCK // CHUNK)
STEPS = 2 * 19
AHEAD = 4
BACKS = 4
LOADS = 5
RING = 4
HEADS = 16
QUADS = 4
CELLS = 16
SLOTS = 9
SHARD = 2 * PARTS * ROWS
BUFFER = BLOCKS * BLOCK

ANY = pl.BlockSpec(memory_space=pl.ANY)
SMEM = pl.BlockSpec(memory_space=pltpu.SMEM)
VMEM = pl.BlockSpec(memory_space=pltpu.VMEM)


def swapped(block, axis, direction):
    return lax.ppermute(block, axis, [(i, i ^ direction) for i in range(lax.axis_size(axis))])


def turned(block, distance):
    devices = lax.axis_size("lon")
    return lax.ppermute(block, "lon", [(i, (i + distance) % devices) for i in range(devices)])


def moved(block, lon_step, lat_step):
    lons, lats = lax.axis_size("lon"), lax.axis_size("lat")
    route = [
        (i * lats + j, (i + lon_step) % lons * lats + (j + lat_step) % lats)
        for i in range(lons)
        for j in range(lats)
    ]
    return lax.ppermute(block, ("lon", "lat"), route)


def gelu_parts(preact):
    argument = TANH_SCALE * (preact + CUBIC_COEF * preact * preact * preact)
    tangent = jnp.tanh(argument)
    activated = 0.5 * preact * (1.0 + tangent)
    derivative = 0.5 * (1.0 + tangent) + 0.5 * preact * (1.0 - tangent * tangent) * TANH_SCALE * (
        1.0 + 3.0 * CUBIC_COEF * preact * preact
    )
    return (activated, derivative)


def norm_rows(field, gain_vec):
    values_f = field.astype(jnp.float32)
    factor = lax.rsqrt(jnp.mean(values_f * values_f, -1, keepdims=True) + EPSILON)
    return values_f * factor * gain_vec


def norm_back(field, gain_vec, grad_in):
    values_f = field.astype(jnp.float32)
    factor = lax.rsqrt(jnp.mean(values_f * values_f, -1, keepdims=True) + EPSILON)
    scaled_grad = grad_in * gain_vec
    inner_mean = jnp.mean(values_f * scaled_grad, -1, keepdims=True)
    return factor * scaled_grad - values_f * factor * factor * factor * inner_mean


def dot_f32(a, b, contract=((1,), (0,))):
    return lax.dot_general(a, b, (contract, ((), ())), preferred_element_type=jnp.float32)


def block_rows(index):
    return pl.ds(pl.multiple_of(index * BLOCK, BLOCK), BLOCK)


def chunk_rows(index):
    return pl.ds(pl.multiple_of(index * CHUNK, CHUNK), CHUNK)


def expert_kernel(place_ref, plan_ref, all_ref, up_own_ref, up_other_ref, down_own_ref, down_other_ref,
                  slots_row_ref, slots_col_ref,
                  back_ref, rows_out_ref, grads_out_ref, hidden_ref, gpre_ref,
                  raw, raw_grad, up, down, rows, grads, result, hidden, gpre, stage, back,
                  raw_sem, raw_grad_sem, weight_sem, rows_sem, grads_sem, hidden_sem, gpre_sem, back_sem):
    def tile(t):
        return pl.ds(t * TILE, TILE)

    def row_loads(n):
        slot = n % LOADS
        return [
            pltpu.make_async_copy(all_ref.at[pl.ds(n * SHARD + first, TILE)], target.at[slot], sem.at[slot])
            for first, target, sem in ((0, raw, raw_sem), (TILE, raw_grad, raw_grad_sem))
        ]

    def begin(n):
        if n < 2 * TILES:
            for load in row_loads(n):
                load.start()

    weight_loads = [
        pltpu.make_async_copy(up_own_ref, up.at[pl.ds(0, 4)], weight_sem.at[0]),
        pltpu.make_async_copy(up_other_ref, up.at[pl.ds(4, 4)], weight_sem.at[1]),
        pltpu.make_async_copy(down_own_ref, down.at[pl.ds(0, 4)], weight_sem.at[2]),
        pltpu.make_async_copy(down_other_ref, down.at[pl.ds(4, 4)], weight_sem.at[3]),
    ]
    for n in range(LOADS):
        begin(n)
    for load in weight_loads:
        load.start()

    def clear(b, carry):
        for buffer in (rows, grads):
            buffer[block_rows(b), :] = jnp.zeros((BLOCK, buffer.shape[1]), buffer.dtype)
        return carry

    result[SPARE * CHUNK : (SPARE + 1) * CHUNK, :] = jnp.zeros((CHUNK, result.shape[1]), result.dtype)
    backs = []
    for h in range(2):
        count = (plan_ref[h, BLOCKS] + 1) // 2 * 2

        def wide_stores(b):
            target = block_rows(h * BLOCKS + b)
            return [
                pltpu.make_async_copy(rows.at[block_rows(b)], rows_out_ref.at[target], rows_sem.at[b]),
                pltpu.make_async_copy(grads.at[block_rows(b)], grads_out_ref.at[target], grads_sem.at[b]),
            ]

        def narrow_stores(b):
            target = block_rows(h * BLOCKS + b)
            return [
                pltpu.make_async_copy(hidden.at[b % RING], hidden_ref.at[target], hidden_sem.at[b % RING]),
                pltpu.make_async_copy(gpre.at[b % RING], gpre_ref.at[target], gpre_sem.at[b % RING]),
            ]

        lax.fori_loop(0, count, clear, 0)
        spots = lax.broadcasted_iota(jnp.int32, (TILE_CHUNKS * CHUNK, TILE), 0)
        for n in range(h * TILES, (h + 1) * TILES):
            pick = (spots == slots_row_ref[n : n + 1, :]).astype(jnp.bfloat16)
            for load, source, buffer in zip(row_loads(n), (raw, raw_grad), (rows, grads)):
                load.wait()
                packed = dot_f32(pick, source[n % LOADS]).astype(jnp.bfloat16)
                for q in range(TILE_CHUNKS):
                    buffer[chunk_rows(place_ref[n, q]), :] = packed[q * CHUNK : (q + 1) * CHUNK]
            begin(n + LOADS)
        if h == 0:
            for load in weight_loads:
                load.wait()

        def step(pair, carry):
            both = (2 * pair, 2 * pair + 1)

            @pl.when(pair >= 2)
            def _():
                for b in both:
                    for store in narrow_stores(b - RING):
                        store.wait()

            preacts = [dot_f32(rows[block_rows(b), :], up[plan_ref[h, b]]) for b in both]
            grad_hiddens = [dot_f32(grads[block_rows(b), :], down[plan_ref[h, b]], ((1,), (1,))) for b in both]
            for b, preact, grad_hidden in zip(both, preacts, grad_hiddens):
                activated, derivative = gelu_parts(preact)
                hidden[b % RING] = activated.astype(jnp.bfloat16)
                grad_pre = (grad_hidden * derivative).astype(jnp.bfloat16)
                gpre[b % RING] = grad_pre
                result[block_rows(b), :] = dot_f32(grad_pre, up[plan_ref[h, b]], ((1,), (1,))).astype(jnp.bfloat16)
                for store in wide_stores(b) + narrow_stores(b):
                    store.start()
            return carry

        lax.fori_loop(0, count // 2, step, 0)

        spots = lax.broadcasted_iota(jnp.int32, (TILE, TILE_CHUNKS * CHUNK), 1)
        for t in range(TILES):
            n = h * TILES + t
            for q in range(TILE_CHUNKS):
                stage[q * CHUNK : (q + 1) * CHUNK, :] = result[chunk_rows(place_ref[n, q]), :]
            pick = (spots == slots_col_ref[:, n : n + 1]).astype(jnp.bfloat16)
            if n >= BACKS:
                backs[n - BACKS].wait()
            back[n % BACKS] = dot_f32(pick, stage[...]).astype(jnp.bfloat16)
            backs.append(pltpu.make_async_copy(back.at[n % BACKS], back_ref.at[tile(n)], back_sem.at[n % BACKS]))
            backs[n].start()

        def finish(b, carry):
            for store in wide_stores(b):
                store.wait()

            @pl.when(b >= count - RING)
            def _():
                for store in narrow_stores(b):
                    store.wait()

            return carry

        lax.fori_loop(0, count, finish, 0)
    for store in backs[-BACKS:]:
        store.wait()


def expert_side(place, plan, rows, ups, downs, slots_row, slots_col):
    features, hidden_units = ups[0].shape[1:]
    wide = jax.ShapeDtypeStruct((2 * BUFFER, features), jnp.bfloat16)
    narrow = jax.ShapeDtypeStruct((2 * BUFFER, hidden_units), jnp.bfloat16)
    blocks_sem, ring_sem = pltpu.SemaphoreType.DMA((BLOCKS,)), pltpu.SemaphoreType.DMA((RING,))
    return pl.pallas_call(
        expert_kernel,
        out_shape=(jax.ShapeDtypeStruct((2 * TILES * TILE, features), jnp.bfloat16), wide, wide, narrow, narrow),
        in_specs=[SMEM] * 2 + [ANY] * 5 + [VMEM, VMEM],
        out_specs=(ANY,) * 5,
        scratch_shapes=[
            pltpu.VMEM((LOADS, TILE, features), jnp.bfloat16),
            pltpu.VMEM((LOADS, TILE, features), jnp.bfloat16),
            pltpu.VMEM((EPG, features, hidden_units), jnp.bfloat16),
            pltpu.VMEM((EPG, hidden_units, features), jnp.bfloat16),
            pltpu.VMEM((BUFFER, features), jnp.bfloat16),
            pltpu.VMEM((BUFFER, features), jnp.bfloat16),
            pltpu.VMEM((BUFFER, features), jnp.bfloat16),
            pltpu.VMEM((RING, BLOCK, hidden_units), jnp.bfloat16),
            pltpu.VMEM((RING, BLOCK, hidden_units), jnp.bfloat16),
            pltpu.VMEM((TILE_CHUNKS * CHUNK, features), jnp.bfloat16),
            pltpu.VMEM((BACKS, TILE, features), jnp.bfloat16),
            pltpu.SemaphoreType.DMA((LOADS,)),
            pltpu.SemaphoreType.DMA((LOADS,)),
            ring_sem,
            blocks_sem,
            blocks_sem,
            ring_sem,
            ring_sem,
            pltpu.SemaphoreType.DMA((BACKS,)),
        ],
        compiler_params=pltpu.CompilerParams(vmem_limit_bytes=52 * 2**20),
        cost_estimate=pl.CostEstimate(flops=30 * 10**9, bytes_accessed=64 * 2**20, transcendentals=2 * 10**6),
    )(place, plan, rows, *ups, *downs, slots_row, slots_col)


def weight_kernel(start_ref, block_ref, *refs):
    arrays, before = refs[:4], refs[4:-8]
    (up_ref, down_ref), buffers, (total, sems) = refs[-8:-6], refs[-6:-2], refs[-2:]
    expert = pl.program_id(0)
    count = start_ref[4]

    def loads(i):
        return [
            pltpu.make_async_copy(a.at[block_rows(block_ref[i])], buffer.at[i % AHEAD], sems.at[n, i % AHEAD])
            for n, (a, buffer) in enumerate(zip(arrays, buffers))
        ]

    def begin(i):
        @pl.when(i < count)
        def _():
            for load in loads(i):
                load.start()

    @pl.when(expert == 0)
    def _():
        for i in range(AHEAD - 1):
            begin(jnp.int32(i))

    total[...] = jnp.zeros_like(total)
    down_ref[...] = before[1][...] if before else jnp.zeros_like(down_ref)

    def step(i, carry):
        for load in loads(i):
            load.wait()
        begin(i + AHEAD - 1)
        rows, grads, hidden, gpre = [buffer[i % AHEAD] for buffer in buffers]
        total[...] += dot_f32(gpre, rows, ((0,), (0,)))
        down_ref[0] += dot_f32(hidden, grads, ((0,), (0,)))
        return carry

    lax.fori_loop(start_ref[expert], start_ref[expert + 1], step, 0)
    up_ref[0] = total[...].T + (before[0][0] if before else 0.0)


def weight_side(plan, arrays, before=()):
    features, hidden_units = arrays[0].shape[1], arrays[2].shape[1]
    up, down = (features, hidden_units), (hidden_units, features)
    outs = tuple(pl.BlockSpec((1, *shape), lambda e: (e, 0, 0)) for shape in (up, down))
    return pl.pallas_call(
        weight_kernel,
        out_shape=tuple(jax.ShapeDtypeStruct((4, *shape), jnp.float32) for shape in (up, down)),
        grid=(4,),
        in_specs=[SMEM] * 2 + [ANY] * 4 + list(outs[: len(before)]),
        out_specs=outs,
        scratch_shapes=[pltpu.VMEM((AHEAD, BLOCK, a.shape[1]), jnp.bfloat16) for a in arrays]
        + [pltpu.VMEM(down, jnp.float32), pltpu.SemaphoreType.DMA((4, AHEAD))],
        compiler_params=pltpu.CompilerParams(vmem_limit_bytes=52 * 2**20),
        cost_estimate=pl.CostEstimate(flops=4 * 10**9, bytes_accessed=25 * 2**20, transcendentals=0),
    )(*plan, *arrays, *before)


def weight_plan(counts, side):
    ahead = lambda v: jnp.cumsum(v) - v
    mine = slice(4 * side, 4 * side + 4)
    halves = [(ahead(c)[mine][None, :] + h * BLOCKS, c[mine][None, :]) for h, c in enumerate(counts)]
    totals = (halves[0][1] + halves[1][1])[0]
    starts = ahead(totals)
    step = jnp.arange(STEPS, dtype=jnp.int32)[:, None]
    inside = (step >= starts[None, :]) & (step < (starts + totals)[None, :])
    offset = step - starts[None, :]
    block = jnp.where(offset >= halves[0][1], halves[1][0] + offset - halves[0][1], halves[0][0] + offset)
    block = jnp.sum(jnp.where(inside, block, 0), 1)
    return (jnp.concatenate([starts, jnp.sum(totals)[None]]).astype(jnp.int32), block.astype(jnp.int32))


def routes(named):
    onehot = (named[..., None] == jnp.arange(EPG)).astype(jnp.bfloat16)
    earlier = jnp.tril(jnp.ones((TILE, TILE), jnp.bfloat16), -1)
    ranks = jnp.einsum("rs,tse->tre", earlier, onehot, preferred_element_type=jnp.float32)
    onehot_f = onehot.astype(jnp.float32)
    rank = jnp.sum(ranks * onehot_f, -1).astype(jnp.int32)
    counts = jnp.sum(onehot_f, 1).astype(jnp.int32)
    chunks = (counts + CHUNK - 1) // CHUNK

    def before(values, axis):
        return jnp.cumsum(values, axis) - values

    starts = before(chunks, 1)
    slots = CHUNK * jnp.sum(onehot_f * starts[:, None, :].astype(jnp.float32), -1).astype(jnp.int32) + rank
    per_block = BLOCK // CHUNK
    blocks = jnp.maximum((jnp.sum(chunks, 0) + per_block - 1) // per_block, 1)
    first_block = before(blocks, 0)
    places = first_block[None, :] * per_block + before(chunks, 0)
    index = jnp.arange(TILE_CHUNKS)[None, :, None]
    inside = (index >= starts[:, None, :]) & (index < (starts + chunks)[:, None, :])
    place = jnp.sum(jnp.where(inside, places[:, None, :] + index - starts[:, None, :] - SPARE, 0), -1) + SPARE
    number = jnp.arange(BLOCKS)[:, None]
    plan = jnp.sum((number >= first_block[None, :]).astype(jnp.int32), -1) - 1
    plan = jnp.concatenate([plan, jnp.sum(blocks)[None]]).astype(jnp.int32)
    return (place.astype(jnp.int32), plan, slots, slots.T, blocks)


def whole(shape):
    return pl.BlockSpec(shape, lambda i: (0,) * len(shape))


def pack_kernel(tokens_ref, cotangent_ref, gain_ref, named_ref, *refs):
    outs, later, scratch = refs[:QUADS], refs[QUADS : 2 * QUADS], refs[2 * QUADS]
    half = WIN // 2
    corners = ((half, half), (half, 0), (0, half), (0, 0))
    for g in range(tokens_ref.shape[0]):
        cotangent_f = cotangent_ref[g].astype(jnp.float32)
        fields = (tokens_ref[g].astype(jnp.float32), gain_ref[g] * cotangent_f, cotangent_f)
        for f, field in enumerate(fields):
            for q, (lon, lat) in enumerate(corners):
                for i in range(half):
                    scratch[f, q, half * i : half * (i + 1), :] = field[lon + i, lat : lat + half, :]
        for q in range(QUADS):
            outs[q][g] = scratch[0, q].astype(jnp.bfloat16)
            outs[q][4 + g] = scratch[1, q].astype(jnp.bfloat16)
            later[q][g] = scratch[2, q].astype(jnp.bfloat16)
    for q in range(QUADS):
        outs[q][SLOTS - 1] = named_ref[q]


def pack(tokens, cotangent, gain, named):
    features = tokens.shape[-1]
    piece = jax.ShapeDtypeStruct((SLOTS, CELLS, features), jnp.bfloat16)
    later = jax.ShapeDtypeStruct((4, CELLS, features), jnp.bfloat16)
    outs = pl.pallas_call(
        pack_kernel,
        out_shape=(piece,) * QUADS + (later,) * QUADS,
        in_specs=[VMEM] * 4,
        out_specs=(VMEM,) * (2 * QUADS),
        scratch_shapes=[pltpu.VMEM((3, QUADS, CELLS, features), jnp.float32)],
        compiler_params=pltpu.CompilerParams(vmem_limit_bytes=52 * 2**20),
    )(tokens, cotangent, gain, named)
    return (outs[:QUADS], outs[QUADS:])


def deal_kernel(where_ref, *refs):
    grads, named, outs = refs[:QUADS], refs[QUADS : 2 * QUADS], refs[2 * QUADS :]
    row = lax.broadcasted_iota(jnp.int32, (CHUNK, 1024), 0)
    for k in range(PARTS):
        group = (where_ref[0] + k) % PARTS
        numbers = jnp.zeros((CHUNK, 1024), jnp.float32)
        for q in range(QUADS):
            outs[k][q * CELLS : (q + 1) * CELLS, :] = grads[q][group]
            line = jnp.sum(jnp.where(row == group, named[q][0].astype(jnp.float32), 0.0), 0, keepdims=True)
            numbers += jnp.where(row == QUADS * k + q, line, 0.0)
        outs[k][ROWS : ROWS + CHUNK, :] = numbers.astype(jnp.bfloat16)


def deal(where, pieces):
    out = jax.ShapeDtypeStruct((ROWS + CHUNK, 1024), jnp.bfloat16)
    return pl.pallas_call(
        deal_kernel,
        out_shape=(out,) * PARTS,
        grid=(1,),
        in_specs=[SMEM]
        + [pl.BlockSpec((4, CELLS, 1024), lambda i: (1, 0, 0))] * QUADS
        + [pl.BlockSpec((1, CELLS, 1024), lambda i: (SLOTS - 1, 0, 0))] * QUADS,
        out_specs=(whole((ROWS + CHUNK, 1024)),) * PARTS,
        compiler_params=pltpu.CompilerParams(vmem_limit_bytes=52 * 2**20),
    )(where, *pieces, *pieces)


def shard_kernel(*refs):
    grads, rows, (out, numbers) = refs[:PARTS], refs[PARTS : 2 * PARTS], refs[2 * PARTS :]
    total = jnp.zeros((CHUNK, 1024), jnp.float32)
    for k in range(PARTS):
        out[k * ROWS : (k + 1) * ROWS, :] = rows[k][...]
        out[(PARTS + k) * ROWS : (PARTS + k + 1) * ROWS, :] = grads[k][:ROWS, :]
        total += grads[k][ROWS:, :].astype(jnp.float32)
    numbers[...] = total[:, :128]


def to_shard(grads, rows):
    return pl.pallas_call(
        shard_kernel,
        out_shape=(
            jax.ShapeDtypeStruct((SHARD, 1024), jnp.bfloat16),
            jax.ShapeDtypeStruct((CHUNK, 128), jnp.float32),
        ),
        in_specs=[VMEM] * (2 * PARTS),
        out_specs=(VMEM, VMEM),
        compiler_params=pltpu.CompilerParams(vmem_limit_bytes=52 * 2**20),
    )(*grads, *rows)


def set_visible(where_ref, visible):
    rows = 4 * ROWS

    def seen(axis):
        cell = lax.broadcasted_iota(jnp.int32, (rows, rows), axis)
        return cell // ROWS * 2 + cell // CELLS % 2 * where_ref[1]

    same = (seen(0) == seen(1)).astype(jnp.float32)
    for i in range(4):
        visible[i * rows : (i + 1) * rows, :] = same


def spread_heads(field):
    head = lax.broadcasted_iota(jnp.int32, field.shape, 1) // HS
    return jnp.concatenate([jnp.where(head == i, field, jnp.zeros_like(field)) for i in range(4)], 0)


def gather_heads(field):
    rows = field.shape[0] // 4
    head = lax.broadcasted_iota(jnp.int32, (rows, field.shape[1]), 1) // HS
    out = field[:rows]
    for i in range(1, 4):
        out = jnp.where(head == i, field[i * rows : (i + 1) * rows], out)
    return out


def softmax_of(projected, visible, quad):
    queries, keyset, values = [projected[:, (c * 4 + quad) * 4 * HS : (c * 4 + quad + 1) * 4 * HS] for c in range(3)]
    queries = spread_heads(queries)
    scores = dot_f32(queries, keyset, ((1,), (1,))) * HS ** (-0.5)
    scores = jnp.where(visible[...] > 0, scores, MASKED)
    weights_exp = jnp.exp(scores - jnp.max(scores, -1, keepdims=True))
    return (queries, keyset, values, weights_exp / jnp.sum(weights_exp, -1, keepdims=True))


def forward_kernel(where_ref, p0, p1, p2, p3, gain1_ref, gain2_ref, win_ref, wout_ref,
                   rolled, projected, middle, n0, n1, n2, n3,
                   win, wout, normed, attended, visible, sems):
    loads = [
        pltpu.make_async_copy(win_ref.at[:, pl.ds(1024 * c, 1024)], win.at[c], sems.at[c]) for c in range(3)
    ] + [pltpu.make_async_copy(wout_ref, wout, sems.at[3])]
    for load in loads:
        load.start()
    set_visible(where_ref, visible)
    for g in range(4):
        for q, piece in enumerate((p0, p1, p2, p3)):
            rolled[g * ROWS + q * CELLS : g * ROWS + (q + 1) * CELLS, :] = piece[g]
        window = slice(g * ROWS, (g + 1) * ROWS)
        normed[window, :] = norm_rows(rolled[window, :], gain1_ref[...]).astype(jnp.bfloat16)
    for c in range(3):
        loads[c].wait()
        projected[:, c * 1024 : (c + 1) * 1024] = dot_f32(normed[...], win[c]).astype(jnp.bfloat16)
    for quad in range(HEADS // 4):
        _, _, values, probs = softmax_of(projected, visible, quad)
        mixed = gather_heads(dot_f32(probs.astype(jnp.bfloat16), values))
        attended[:, quad * 4 * HS : (quad + 1) * 4 * HS] = mixed.astype(jnp.bfloat16)
    loads[3].wait()
    produced = dot_f32(attended[...], wout[...]).astype(jnp.bfloat16)
    for g in range(4):
        window = slice(g * ROWS, (g + 1) * ROWS)
        total = rolled[window, :].astype(jnp.float32) + produced[window, :].astype(jnp.float32)
        middle[window, :] = total.astype(jnp.bfloat16)
        normed[window, :] = norm_rows(middle[window, :], gain2_ref[...]).astype(jnp.bfloat16)
    for k, out in enumerate((n0, n1, n2, n3)):
        group = (where_ref[0] + k) % PARTS
        out[...] = normed[pl.ds(pl.multiple_of(group * ROWS, ROWS), ROWS), :]


def attention_forward(where, pieces, gain1, gain2, weight_in, weight_out):
    rows = 4 * ROWS
    field = jax.ShapeDtypeStruct((rows, 1024), jnp.bfloat16)
    part = jax.ShapeDtypeStruct((ROWS, 1024), jnp.bfloat16)
    return pl.pallas_call(
        forward_kernel,
        out_shape=(field, jax.ShapeDtypeStruct((rows, 3072), jnp.bfloat16), field) + (part,) * PARTS,
        grid=(1,),
        in_specs=[SMEM]
        + [whole((4, CELLS, 1024))] * QUADS
        + [whole((1, 1024))] * 2
        + [ANY, ANY],
        out_specs=(whole((rows, 1024)), whole((rows, 3072)), whole((rows, 1024))) + (whole((ROWS, 1024)),) * PARTS,
        scratch_shapes=[
            pltpu.VMEM((3, 1024, 1024), jnp.bfloat16),
            pltpu.VMEM((1024, 1024), jnp.bfloat16),
            pltpu.VMEM((rows, 1024), jnp.bfloat16),
            pltpu.VMEM((rows, 1024), jnp.bfloat16),
            pltpu.VMEM((4 * rows, rows), jnp.float32),
            pltpu.SemaphoreType.DMA((4,)),
        ],
        compiler_params=pltpu.CompilerParams(vmem_limit_bytes=52 * 2**20),
        cost_estimate=pl.CostEstimate(flops=4 * 10**9, bytes_accessed=14 * 2**20, transcendentals=2**20),
    )(where, *pieces, gain1, gain2, weight_in, weight_out)


def backward_kernel(where_ref, r0, r1, r2, r3, c0, c1, c2, c3, middle, rolled, projected, gain1_ref, gain2_ref,
                    win_ref, wout_ref, o0, o1, o2, o3,
                    win, wout, arrived, grad_middle, grad_att, grad_proj, visible, sems):
    loads = [
        pltpu.make_async_copy(win_ref.at[:, pl.ds(1024 * c, 1024)], win.at[c], sems.at[c]) for c in range(3)
    ] + [pltpu.make_async_copy(wout_ref, wout, sems.at[3])]
    for load in loads[::-1]:
        load.start()
    set_visible(where_ref, visible)
    for k, part in enumerate((r0, r1, r2, r3)):
        group = (where_ref[0] + k) % PARTS
        arrived[pl.ds(pl.multiple_of(group * ROWS, ROWS), ROWS), :] = part[...]
    for g in range(4):
        window = slice(g * ROWS, (g + 1) * ROWS)
        cotangent = jnp.concatenate([c[g] for c in (c0, c1, c2, c3)], 0).astype(jnp.float32)
        back = norm_back(middle[window, :], gain2_ref[...], arrived[window, :].astype(jnp.float32))
        grad_middle[window, :] = (cotangent + back).astype(jnp.bfloat16)
    loads[3].wait()
    grad_att[...] = dot_f32(grad_middle[...], wout[...], ((1,), (1,))).astype(jnp.bfloat16)
    for quad in range(HEADS // 4):
        queries, keyset, values, probs = softmax_of(projected, visible, quad)
        grad_heads = spread_heads(grad_att[:, quad * 4 * HS : (quad + 1) * 4 * HS])
        grad_probs = dot_f32(grad_heads, values, ((1,), (1,)))
        grad_scores = probs * (grad_probs - jnp.sum(probs * grad_probs, -1, keepdims=True))
        scaled = (grad_scores * HS ** (-0.5)).astype(jnp.bfloat16)
        grads = (
            gather_heads(dot_f32(scaled, keyset)),
            dot_f32(scaled, queries, ((0,), (0,))),
            dot_f32(probs.astype(jnp.bfloat16), grad_heads, ((0,), (0,))),
        )
        for c in range(3):
            start = (c * 4 + quad) * 4 * HS
            grad_proj[:, start : start + 4 * HS] = grads[c].astype(jnp.bfloat16)
    for load in loads[:3]:
        load.wait()
    grad_norm = sum(
        dot_f32(grad_proj[:, c * 1024 : (c + 1) * 1024], win[c], ((1,), (1,))) for c in range(3)
    )
    for g in range(4):
        window = slice(g * ROWS, (g + 1) * ROWS)
        branch = norm_back(rolled[window, :], gain1_ref[...], grad_norm[window, :]).astype(jnp.bfloat16)
        total = grad_middle[window, :].astype(jnp.float32) + branch.astype(jnp.float32)
        for q, out in enumerate((o0, o1, o2, o3)):
            out[g] = total[q * CELLS : (q + 1) * CELLS, :].astype(jnp.bfloat16)


def attention_backward(where, returned, pieces, middle, rolled, projected, gain1, gain2, weight_in, weight_out):
    rows = 4 * ROWS
    piece = jax.ShapeDtypeStruct((4, CELLS, 1024), jnp.bfloat16)
    return pl.pallas_call(
        backward_kernel,
        out_shape=(piece,) * QUADS,
        grid=(1,),
        in_specs=[SMEM]
        + [whole((ROWS, 1024))] * PARTS
        + [whole((4, CELLS, 1024))] * QUADS
        + [whole((rows, 1024))] * 2
        + [whole((rows, 3072))]
        + [whole((1, 1024))] * 2
        + [ANY, ANY],
        out_specs=(whole((4, CELLS, 1024)),) * QUADS,
        scratch_shapes=[
            pltpu.VMEM((3, 1024, 1024), jnp.bfloat16),
            pltpu.VMEM((1024, 1024), jnp.bfloat16),
            pltpu.VMEM((rows, 1024), jnp.bfloat16),
            pltpu.VMEM((rows, 1024), jnp.bfloat16),
            pltpu.VMEM((rows, 1024), jnp.bfloat16),
            pltpu.VMEM((rows, 3072), jnp.bfloat16),
            pltpu.VMEM((4 * rows, rows), jnp.float32),
            pltpu.SemaphoreType.DMA((4,)),
        ],
        compiler_params=pltpu.CompilerParams(vmem_limit_bytes=52 * 2**20),
        cost_estimate=pl.CostEstimate(flops=6 * 10**9, bytes_accessed=14 * 2**20, transcendentals=2**20),
    )(where, *returned, *pieces, middle, rolled, projected, gain1, gain2, weight_in, weight_out)


def roll_out(pieces):
    half = WIN // 2
    stays, lat_part, lon_part, both = pieces
    shape = (pieces[0].shape[0], half, half, pieces[0].shape[-1])
    grid = lambda a: a.reshape(shape)
    upper = jnp.concatenate([grid(both), grid(lon_part)], 2)
    lower = jnp.concatenate([grid(lat_part), grid(stays)], 2)
    return jnp.concatenate([upper, lower], 1)


def spread(blocks):
    return [blocks[0]] + [turned(blocks[k], 2 * k) for k in range(1, PARTS)]


def body(
    tokens,
    cotangent,
    attention_in,
    attention_out,
    norm_attention,
    norm_expert,
    expert_up,
    expert_down,
    route_gain,
    assignment,
    slot_index,
):
    groups_n, lon_rows, lat_rows, features = tokens.shape
    lat_count = lax.axis_size("lat")
    lon_index = lax.axis_index("lon")
    lat_index = lax.axis_index("lat")
    place, core = lon_index // 2, lon_index % 2
    where = jnp.stack([place, (lat_index == lat_count - 1).astype(place.dtype)]).astype(jnp.int32)
    gain1, gain2 = norm_attention[None, :], norm_expert[None, :]

    half = WIN // 2
    named = assignment.reshape(groups_n, 2, half, 2, half).transpose(1, 3, 0, 2, 4)[::-1, ::-1]
    named = named.reshape(QUADS, groups_n, CELLS).astype(jnp.bfloat16)
    named = jnp.pad(named, ((0, 0), (0, CHUNK - groups_n), (0, features - CELLS)))
    def roll_in(parts):
        return (parts[0], moved(parts[1], 0, -1), moved(parts[2], -1, 0), moved(parts[3], -1, -1))

    first, later = pack(tokens, cotangent, route_gain[..., None], named)
    first = roll_in(first)
    dealt = deal(where, first)
    first, dealt = lax.optimization_barrier((first, dealt))
    grads = spread(dealt)

    rolled, projected, middle, *normed = attention_forward(
        where, first, gain1, gain2, attention_in, attention_out
    )
    normed, grads = lax.optimization_barrier((normed, grads))
    shard, numbers = to_shard(grads, spread(normed))
    rows = lax.all_gather(shard, "lat", axis=0, tiled=True)

    numbers, expert_down, expert_up, later = lax.optimization_barrier((numbers, expert_down, expert_up, later))
    ups, downs = (expert_up, swapped(expert_up, "lon", 1)), (expert_down, swapped(expert_down, "lon", 1))
    later = roll_in(later)

    numbers, later = lax.optimization_barrier((numbers, later))
    numbers = lax.all_gather(numbers.astype(jnp.int32), "lat", axis=0)
    numbers = numbers[:, :, :CELLS].reshape(lat_count, PARTS * ROWS) ^ (4 * core)
    places, plans, slots, slots_t, counts = zip(*[routes(numbers[TILES * h : TILES * (h + 1)]) for h in range(2)])

    back, *arrays = expert_side(
        jnp.concatenate(places, 0), jnp.stack(plans), rows, ups, downs,
        jnp.concatenate(slots, 0), jnp.concatenate(slots_t, 1),
    )
    summed = lax.psum_scatter(back, "lat", scatter_dimension=0, tiled=True)
    came = [swapped(a, "lon", 1) for a in weight_side(weight_plan(counts, 1), arrays)]
    grad_up, grad_down = weight_side(weight_plan(counts, 0), arrays, came)

    summed, grad_up, grad_down = lax.optimization_barrier((summed, grad_up, grad_down))
    summed = [summed[k * ROWS : (k + 1) * ROWS] for k in range(PARTS)]
    returned = [summed[0]] + [turned(summed[k], -2 * k) for k in range(1, PARTS)]
    out = attention_backward(
        where, returned, later, middle, rolled, projected, gain1, gain2, attention_in, attention_out
    )
    came = [moved(out[1], 0, 1), moved(out[2], 1, 0), moved(out[3], 1, 1)]
    return (roll_out([out[0], *came]), grad_up, grad_down)


def solution(mesh):
    return jax.shard_map(
        body,
        mesh=mesh,
        in_specs=(
            P(None, "lon", "lat", None),
            P(None, "lon", "lat", None),
            P(),
            P(),
            P(),
            P(),
            P("lon", None, "lat"),
            P("lon", "lat", None),
            P(None, "lon", "lat"),
            P(None, "lon", "lat"),
            P(None, "lon", "lat"),
        ),
        out_specs=(P(None, "lon", "lat", None), P("lon", None, "lat"), P("lon", "lat", None)),
        check_vma=False,
    )
```
